512 devices in a mesh: section: 16 (over x, z_hi, core), dp: 32 (over y, z_lo).
Axes of the slice: x: 4, y: 4, z: 16 (z_hi: 2, z_lo: 8; z = z_hi * 8 + z_lo), core: 2. Of those that a mesh axis runs over, the one named last changes fastest.
Arguments:
- section_inputs: bfloat16 [16, 2, 2048, 4096], P('section', None, 'dp'), may hold values from -6 to 6
- loss_grads: bfloat16 [2, 2048, 4096], P(None, 'dp'), may hold values from -384 to 384
- weight_codes: int32 [2, 2048], P(None, 'dp'), may hold values from 0 to 127, as said below
- proj_weight: bfloat16 [16, 4096, 512], P('section', 'dp'), may hold values from -0.09375 to 0.09375
Outputs:
- weight_grads: float32 [16, 4096, 512], P('section', 'dp')
The draws below stay inside these ranges and needn't reach their ends.
Inputs may be any that keep to these rules, and one draw needn't show every extreme that they name: `weight_codes`: the weight of a token is its code / 127.
All inputs are finite; a program needn't handle non-finite values.
Results may differ from the reference program's by a relative error of at most 0.035.
Values may be sent and summed in bfloat16 or wider, within the bound.
A program may use at most 128 MiB of HBM per device.

```python
import jax
import jax.numpy as jnp
from jax import lax

D = 4096
K = 512
TOK_DEV = 64
MB = 2
TOKENS = 2048
N_SECTION = 16
N_DP = 32


def draw_weight_codes(key, part):
    key = jax.random.fold_in(key, 11)
    level_key, block_key, code_key = jax.random.split(key, 3)
    positions = jnp.arange(TOKENS, dtype=jnp.int32)
    ramp = 32 + 95 * positions // max(TOKENS - 1, 1)
    overall = jax.random.randint(level_key, (), 8, 128, dtype=jnp.int32)
    blocks = jax.random.randint(block_key, (TOKENS // TOK_DEV,), 64, 128, dtype=jnp.int32)
    block_level = jnp.repeat(blocks, TOK_DEV)
    ceiling = jnp.clip(overall * block_level * ramp // (127 * 128), 1, 127)
    codes = jax.random.randint(code_key, (MB, TOKENS), 0, ceiling[None, :] + 1, dtype=jnp.int32)
    codes = codes.at[0, TOKENS - 1].set(127)
    codes = codes.at[MB - 1, 0].set(0)
    return codes


def shard_levels(rng, extent, shards, low, high):
    factor_of = 1.0
    for dim, blocks in shards:
        steps = jax.random.uniform(jax.random.fold_in(jax.random.fold_in(rng, 6), dim), (blocks,), jnp.float32, low / len(shards), high / len(shards))
        factor_of = factor_of * jnp.repeat(jnp.exp(steps), extent[dim] // blocks).reshape((-1,) + (1,) * (len(extent) - 1 - dim))
    return factor_of


def noise(key, shape, spread, most, pieces=(), held_as=jnp.bfloat16):
    drawn = jax.random.normal(key, shape, jnp.float32) * spread
    if len(pieces) > 0:
        drawn = shard_levels(key, shape, pieces, -0.22, 0.18) * drawn
    return jnp.clip(drawn, min=-most, max=most).astype(held_as)


def setup_inputs(seed: int = 0) -> dict:
    keys = jax.random.split(jax.random.key(seed), 5)
    return {
        "section_inputs": noise(keys[0], (N_SECTION, MB, TOKENS, D), 1.0, 6.0, ((0, 16), (2, 32))),
        "loss_grads": noise(keys[1], (MB, TOKENS, D), ((MB * TOKENS) ** 0.5), 384.0, ((1, 32),)),
        "weight_codes": draw_weight_codes(jax.random.fold_in(keys[4], 71), 0),
        "proj_weight": noise(keys[3], (N_SECTION, D, K), D ** -0.5, 0.09375, ((0, 16), (1, 32))),
    }


epsilon = 1e-06

def section_backward(inputs, grad_output, weight):
    values = inputs.astype(jnp.float32)
    inv_rms = lax.rsqrt(lax.optimization_barrier(jnp.mean(values * values, axis=-1, keepdims=True)) + epsilon)
    unit_rows = values * inv_rms
    normed = unit_rows.astype(jnp.bfloat16)
    project = jnp.dot(normed, weight, preferred_element_type=jnp.float32)
    activated = jax.nn.silu(project).astype(jnp.bfloat16)
    grad_act = jnp.dot(grad_output, weight, preferred_element_type=jnp.float32)
    gate_prob = jax.nn.sigmoid(project)
    grad_proj = (grad_act * gate_prob * (1.0 + project * (1.0 - gate_prob))).astype(jnp.bfloat16)
    grad_norm = lax.dot_general(grad_proj, weight, (((1,), (1,)), ((), ())), preferred_element_type=jnp.float32)
    grad_rows = inv_rms * (grad_norm - unit_rows * lax.optimization_barrier(jnp.mean(grad_norm * unit_rows, axis=-1, keepdims=True)))
    grad_input = (grad_output.astype(jnp.float32) + grad_rows).astype(jnp.bfloat16)
    return (grad_input, normed, grad_proj, activated)

def weight_term(normed, grad_proj, grad_output, activated):
    dims = (((0,), (0,)), ((), ()))
    first = lax.dot_general(normed, grad_proj, dims, preferred_element_type=jnp.float32)
    return first + lax.dot_general(grad_output, activated, dims, preferred_element_type=jnp.float32)

def reference(section_inputs, loss_grads, weight_codes, proj_weight):
    code_values = weight_codes.astype(jnp.float32)
    weight_total = jnp.sum(code_values) / 127.0
    seed_grads = (loss_grads.astype(jnp.float32) * (code_values / 127.0)[:, :, None] / weight_total).astype(jnp.bfloat16)

    def one_section(carried, pair):
        inputs, weight = pair
        flat_in = inputs.reshape(MB * TOKENS, D)
        flat_out = carried.reshape(MB * TOKENS, D)
        grad_input, normed, grad_proj, activated = section_backward(flat_in, flat_out, weight)
        normed = normed.reshape(MB, TOKENS, D)
        outs = carried
        grad_proj = grad_proj.reshape(MB, TOKENS, K)
        activated = activated.reshape(MB, TOKENS, K)

        def add_group(group, total):
            start = (group * TOK_DEV).astype(jnp.int32)
            pick_norm = lax.dynamic_slice_in_dim(normed, start, TOK_DEV, 1).reshape(MB * TOK_DEV, D)
            pick_outs = lax.dynamic_slice_in_dim(outs, start, TOK_DEV, 1).reshape(MB * TOK_DEV, D)
            pick_proj = lax.dynamic_slice_in_dim(grad_proj, start, TOK_DEV, 1).reshape(MB * TOK_DEV, K)
            pick_act = lax.dynamic_slice_in_dim(activated, start, TOK_DEV, 1).reshape(MB * TOK_DEV, K)
            term = weight_term(pick_norm, pick_proj, pick_outs, pick_act)
            rounded = lax.optimization_barrier(term.astype(jnp.bfloat16)).astype(jnp.float32)
            return total + rounded
        summed = lax.fori_loop(0, N_DP, add_group, jnp.zeros((D, K), jnp.float32))
        return (grad_input.reshape(MB, TOKENS, D), summed)
    unused, grads = lax.scan(one_section, seed_grads, (section_inputs, proj_weight), reverse=True)
    return grads
```

```python
import jax
import jax.numpy as jnp
from jax import lax
from jax.experimental import pallas as pl
from jax.experimental.pallas import tpu as pltpu
from jax.sharding import PartitionSpec as P

MESH = pl.DeviceIdType.MESH
F32 = jnp.float32
BF16 = jnp.bfloat16
EPSILON = 1e-06
TOK = 64
WIDTH = 4096
HIDDEN = 512
ROWS = 128
CHUNKS = 8
COLS = WIDTH // CHUNKS
GROUPS = COLS // ROWS


def device(x, z, core, y):
    return (x * 4 + (z // 8) * 2 + core, y * 8 + z % 8)


def kernel(
    inputs, loss, codes, shard, out,
    weights, units, normed, grads, outgoing, factors, project, slope, inv_rms, partial,
    hop1, hop2p, hop2m, ringp, ringm, final, tally, tally_in, staged,
    local_sem, gather_recv, gather_z_send, gather_y_send, cross_send, cross_recv,
    chain_send, chain_recv, hop1_recv, hop2p_recv, hop2m_recv, ringp_recv, ringm_recv,
    sum_y_send, sum_z_send, final_send, final_recv, tally_send, tally_recv,
):
    section = lax.axis_index("section")
    group = lax.axis_index("dp")
    x, half, core = section // 4, (section // 2) % 2, section % 2
    y, low = group // 8, group % 8
    z = half * 8 + low
    sister = device(x, z, 1 - core, y)
    zdev = {s: device(x, (z + 16 + s) % 16, core, y) for s in (1, -1, 2, -2, 4, -4)}
    ydev = {s: device(x, z, core, (y + 4 + s) % 4) for s in (1, -1, 2)}
    home = core == half
    first = jnp.logical_and(x == 3, core == 1)
    last = jnp.logical_and(x == 0, core == 0)
    far = (z + 8) % 16
    next_x = device((x + 3) % 4, z, 1, y)
    prev_x = device((x + 1) % 4, z, 0, y)

    barrier = pltpu.get_barrier_semaphore()

    def greet(target):
        pl.semaphore_signal(barrier, inc=1, device_id=target, device_id_type=MESH)

    for s in (1, -1, 2, 4):
        greet(zdev[s])
    for s in (1, -1, 2):
        greet(ydev[s])
    greet(sister)

    @pl.when(jnp.logical_not(home))
    def _():
        greet(device(x, far, 0, y))
        greet(device(x, far, 1, y))

    @pl.when(jnp.logical_and(core == 1, x < 3))
    def _():
        greet(prev_x)

    pl.semaphore_wait(barrier, 9 + (1 - core) * ((x + 3) // 4))

    def remote(src, dst, send, recv, target):
        return pltpu.make_async_remote_copy(
            src_ref=src, dst_ref=dst, send_sem=send, recv_sem=recv,
            device_id=target, device_id_type=MESH,
        )

    here = y * 8 + low

    def own_weight():
        return pltpu.make_async_copy(shard.at[0], weights.at[core, here], local_sem.at[0])

    def lend_weight():
        return remote(
            shard.at[0], weights.at[core, here], cross_send.at[0],
            gather_recv.at[core, here], sister,
        )

    def own_inputs():
        return pltpu.make_async_copy(inputs.at[0, half], units.at[core], local_sem.at[1])

    def lend_inputs():
        return remote(
            inputs.at[0, half], units.at[core], cross_send.at[1], cross_recv.at[core], sister
        )

    def cross_inputs():
        return remote(
            inputs.at[0, 1 - half], units.at[core], cross_send.at[2], cross_recv.at[core],
            device(x, far, half, y),
        )

    def seed_copy():
        return pltpu.make_async_copy(loss.at[half], staged, local_sem.at[2])

    @pl.when(home)
    def _():
        own_weight().start()
        own_inputs().start()

    @pl.when(jnp.logical_not(home))
    def _():
        lend_weight().start()
        lend_inputs().start()

    cross_inputs().start()
    seed_copy().start()

    def block_ref(k, yy, ll):
        return weights.at[k, yy * 8 + ll]

    def gather_z(k, ll, sgn):
        return remote(
            block_ref(k, y, ll), block_ref(k, y, ll), gather_z_send.at[(1 - sgn) // 2, k, ll],
            gather_recv.at[k, y * 8 + ll], zdev[sgn],
        )

    def gather_y(k, yy, ll, sgn, slot):
        return remote(
            block_ref(k, yy, ll), block_ref(k, yy, ll), gather_y_send.at[slot, k, ll],
            gather_recv.at[k, yy * 8 + ll], ydev[sgn],
        )

    def arrived(k, yy, ll):
        remote(
            block_ref(k, yy, ll), block_ref(k, yy, ll), cross_send.at[0],
            gather_recv.at[k, yy * 8 + ll], sister,
        ).wait_recv()

    def side(ll):
        return 1 - 2 * (ll % 2)

    def ring_place(t, sgn):
        zz = (z + 16 - sgn * t) % 16
        return zz // 8 == core, zz % 8

    def spread_y(k, ll):
        gather_y(k, y, ll, 1, 0).start()
        gather_y(k, y, ll, -1, 1).start()

    @pl.when(home)
    def _():
        own_weight().wait()

        def begin(k):
            for sgn in (1, -1):
                gather_z(k, low, sgn).start()
            spread_y(k, low)

        begin(core)
        arrived(1 - core, y, low)
        begin(1 - core)

    def relay_y(t, sgn):
        valid, ll = ring_place(t, sgn)
        valid = jnp.logical_and(valid, jnp.logical_or(t < 8, side(ll) == sgn))

        @pl.when(valid)
        def _():
            for k in (1, 0):
                arrived(k, (y + 3) % 4, ll)

                @pl.when(side(ll) == 1)
                def _():
                    gather_y(k, (y + 3) % 4, ll, 1, 2).start()

                arrived(k, (y + 1) % 4, ll)

                @pl.when(side(ll) == -1)
                def _():
                    gather_y(k, (y + 1) % 4, ll, -1, 2).start()

    def relay_z(t, sgn):
        valid, ll = ring_place(t, sgn)
        valid = jnp.logical_and(valid, jnp.logical_or(t < 8, side(ll) == sgn))
        onward = jnp.logical_or(t < 7, jnp.logical_and(t == 7, side(ll) == sgn))

        @pl.when(valid)
        def _():
            for k in (1, 0):
                arrived(k, y, ll)

                @pl.when(onward)
                def _():
                    gather_z(k, ll, sgn).start()

                spread_y(k, ll)

    def gather_step(t, carry):
        for sgn in (1, -1):
            relay_z(t, sgn)

        @pl.when(t == 1)
        def _():
            relay_y(0, 1)

        @pl.when(t > 1)
        def _():
            for sgn in (1, -1):
                relay_y(t - 1, sgn)

        return carry

    lax.fori_loop(1, 9, gather_step, 0)
    for sgn in (1, -1):
        relay_y(8, sgn)

    tally[0] = jnp.broadcast_to(
        jnp.sum(codes[0] + codes[1], axis=0, keepdims=True), (8, 128)
    )
    for i, target in enumerate((zdev[-1], zdev[-2], zdev[-4], ydev[-1], ydev[2])):
        copy = remote(tally.at[i], tally_in.at[i], tally_send.at[i], tally_recv.at[i], target)
        copy.start()
        copy.wait()
        tally[i + 1] = tally[i] + tally_in[i]

    seed_copy().wait()

    @pl.when(first)
    def _():
        scale = codes[half, :, 0:1] / 127.0
        for j in range(CHUNKS):
            part = staged[:, j * COLS:(j + 1) * COLS].astype(F32)
            grads[1, j] = (part * scale).astype(BF16)

    @pl.when(home)
    def _():
        own_inputs().wait()

    def inputs_arrived(k):
        remote(
            units.at[k], units.at[k], cross_send.at[1], cross_recv.at[k], sister
        ).wait_recv()

    @pl.when(home)
    def _():
        inputs_arrived(1 - core)

    @pl.when(jnp.logical_not(home))
    def _():
        inputs_arrived(0)
        inputs_arrived(1)

    def far_arrived(ll, carry):
        for k in (1, 0):
            arrived(k, (y + 2) % 4, ll)
        return carry

    lax.fori_loop(0, 8, far_arrived, 0)

    def weight_chunk(k, j):
        return weights[k, pl.ds(j * GROUPS, GROUPS)].reshape(COLS, HIDDEN)

    def columns(ref, k, j):
        return ref[k, :, pl.ds(pl.multiple_of(j * COLS, COLS), COLS)]

    def prepare(k):
        def square(j, acc):
            v = columns(units, k, j).astype(F32)
            return acc + jnp.sum(v * v, axis=-1, keepdims=True)

        total = lax.fori_loop(0, CHUNKS, square, jnp.zeros((TOK, 1), F32))
        inv = lax.rsqrt(total / WIDTH + EPSILON)
        inv_rms[k] = jnp.broadcast_to(inv, (TOK, 128))

        def multiply(j, acc):
            row = (columns(units, k, j).astype(F32) * inv).astype(BF16)
            normed[k, :, pl.ds(pl.multiple_of(j * COLS, COLS), COLS)] = row
            return acc + jnp.dot(row, weight_chunk(k, j), preferred_element_type=F32)

        value = lax.fori_loop(0, CHUNKS, multiply, jnp.zeros((TOK, HIDDEN), F32))
        prob = jax.nn.sigmoid(value)
        project[k] = value
        slope[k] = prob * (1.0 + value * (1.0 - prob))
        factors[k, TOK:] = (value * prob).astype(BF16)

    for k in (1, 0):
        prepare(k)

    def chain(j, target):
        return remote(outgoing.at[j], grads.at[1, j], chain_send.at[j], chain_recv.at[j], target)

    def stage(k):
        def act_grad(j, acc):
            if k == 1:
                @pl.when(jnp.logical_not(first))
                def _():
                    chain(j, sister).wait_recv()
            return acc + jnp.dot(grads[k, j], weight_chunk(k, j), preferred_element_type=F32)

        grad_act = lax.fori_loop(0, CHUNKS, act_grad, jnp.zeros((TOK, HIDDEN), F32))
        grad_proj = (grad_act * slope[k]).astype(BF16)
        factors[k, :TOK] = grad_proj
        mean = jnp.sum(grad_proj.astype(F32) * project[k], axis=-1, keepdims=True) / WIDTH
        inv = inv_rms[k, :, 0:1]

        def in_grad(j, carry):
            norm = lax.dot_general(
                grad_proj, weight_chunk(k, j), (((1,), (1,)), ((), ())),
                preferred_element_type=F32,
            )
            unit = columns(units, k, j).astype(F32) * inv
            result = (grads[k, j].astype(F32) + inv * (norm - unit * mean)).astype(BF16)
            if k == 1:
                grads[0, j] = result
            else:
                outgoing[j] = result

                @pl.when(core == 1)
                def _():
                    chain(j, sister).start()

                @pl.when(core == 0)
                def _():
                    chain(j, next_x).start()

            return carry

        def onward():
            lax.fori_loop(0, CHUNKS, in_grad, 0)

        if k == 1:
            onward()
        else:
            pl.when(jnp.logical_not(last))(onward)

    stage(1)
    stage(0)

    def weight_grad(k):
        def rows(j, carry):
            left = jnp.concatenate([columns(normed, k, j), grads[k, j]], axis=0)
            term = lax.dot_general(
                left, factors[k], (((0,), (0,)), ((), ())), preferred_element_type=F32
            )
            partial[k, pl.ds(j * GROUPS, GROUPS)] = term.astype(BF16).reshape(
                GROUPS, ROWS, HIDDEN
            )
            return carry

        lax.fori_loop(0, CHUNKS, rows, 0)

    def part_ref(k, dy, ll):
        return partial.at[k, ((y + 4 + dy) % 4) * 8 + ll]

    def send_hop1(k, ll, sgn):
        return remote(
            part_ref(k, 2, ll), hop1.at[k, ll], sum_y_send.at[0, k, ll], hop1_recv.at[k, ll],
            ydev[sgn],
        )

    def send_hop2(k, ll, sgn):
        land, sem = (hop2p, hop2p_recv) if sgn == 1 else (hop2m, hop2m_recv)
        return remote(
            part_ref(k, sgn, ll), land.at[k, ll], sum_y_send.at[(3 - sgn) // 2, k, ll],
            sem.at[k, ll], ydev[sgn],
        )

    def send_ring(k, ll, sgn):
        land, sem = (ringp, ringp_recv) if sgn == 1 else (ringm, ringm_recv)
        return remote(
            part_ref(k, 0, ll), land.at[k, ll], sum_z_send.at[k, ll], sem.at[k, ll], zdev[sgn]
        )

    def target_place(t, sgn):
        zz = (z + 16 + sgn * t) % 16
        ll = zz % 8
        valid = jnp.logical_and(zz // 8 == core, jnp.logical_or(t < 8, side(ll) == sgn))
        return valid, ll

    def begin_y(k, t, sgn):
        valid, ll = target_place(t, sgn)

        @pl.when(valid)
        def _():
            @pl.when(side(ll) == 1)
            def _():
                send_hop1(k, ll, 1).start()
                send_hop2(k, ll, -1).start()

            @pl.when(side(ll) == -1)
            def _():
                send_hop1(k, ll, -1).start()
                send_hop2(k, ll, 1).start()

    def begin_sum(k):
        def body(i, carry):
            for sgn in (1, -1):
                begin_y(k, 8 - i, sgn)
            return carry

        lax.fori_loop(0, 8, body, 0)
        begin_y(k, 0, 1)

    def add_into(k, dy, ll, extra):
        index = ((y + 4 + dy) % 4) * 8 + ll
        value = partial[k, index].astype(F32)
        for ref in extra:
            value = value + ref[k, ll].astype(F32)
        partial[k, index] = value.astype(BF16)

    def middle_y(t, sgn):
        valid, ll = target_place(t, sgn)

        @pl.when(valid)
        def _():
            for k in (1, 0):
                send_hop1(k, ll, 1).wait_recv()

                @pl.when(side(ll) == 1)
                def _():
                    add_into(k, 1, ll, (hop1,))
                    send_hop2(k, ll, 1).start()

                @pl.when(side(ll) == -1)
                def _():
                    add_into(k, -1, ll, (hop1,))
                    send_hop2(k, ll, -1).start()

    def ring_sum(t, sgn):
        valid, ll = target_place(t, sgn)
        fed = jnp.logical_or(t < 7, jnp.logical_and(t == 7, side(ll) == sgn))
        land = ringp if sgn == 1 else ringm

        @pl.when(valid)
        def _():
            for k in (1, 0):
                send_hop2(k, ll, 1).wait_recv()
                send_hop2(k, ll, -1).wait_recv()

                @pl.when(fed)
                def _():
                    send_ring(k, ll, sgn).wait_recv()
                    add_into(k, 0, ll, (hop2p, hop2m, land))

                @pl.when(jnp.logical_not(fed))
                def _():
                    add_into(k, 0, ll, (hop2p, hop2m))

                send_ring(k, ll, sgn).start()

    for k in (1, 0):
        weight_grad(k)
        begin_sum(k)

    def sum_step(i, carry):
        @pl.when(i < 8)
        def _():
            for sgn in (1, -1):
                middle_y(8 - i, sgn)

        @pl.when(i == 8)
        def _():
            middle_y(0, 1)

        @pl.when(jnp.logical_and(i >= 1, i < 9))
        def _():
            for sgn in (1, -1):
                ring_sum(9 - i, sgn)

        return carry

    lax.fori_loop(0, 9, sum_step, 0)

    scale = 127.0 / tally[5, 0:1, 0:1]

    def send_final():
        return remote(final.at[0], final.at[1], final_send.at[0], final_recv.at[0], sister)

    @pl.when(home)
    def _():
        def total(k):
            for sgn in (1, -1):
                send_hop2(k, low, sgn).wait_recv()
                send_ring(k, low, sgn).wait_recv()
            value = partial[k, here].astype(F32)
            for ref in (hop2p, hop2m, ringp, ringm):
                value = value + ref[k, low].astype(F32)
            return value

        final[0] = total(1 - core)
        send_final().start()
        out[0] = total(core) * scale
        send_final().wait_send()

    @pl.when(jnp.logical_not(home))
    def _():
        send_final().wait_recv()
        out[0] = final[1] * scale

    @pl.when(jnp.logical_not(home))
    def _():
        lend_weight().wait_send()
        lend_inputs().wait_send()

    cross_inputs().wait_send()

    @pl.when(jnp.logical_not(last))
    def _():
        for j in range(CHUNKS):
            chain(j, sister).wait_send()

    def settle(ll, carry):
        zz = core * 8 + ll
        ahead = (z + 16 - zz) % 16
        plus = jnp.logical_or(ahead < 7, jnp.logical_and(ahead == 7, side(ll) == 1))
        back = (16 - ahead) % 16
        minus = jnp.logical_or(back < 7, jnp.logical_and(back == 7, side(ll) == -1))
        for k in (1, 0):
            @pl.when(plus)
            def _():
                gather_z(k, ll, 1).wait_send()

            @pl.when(minus)
            def _():
                gather_z(k, ll, -1).wait_send()

            gather_y(k, y, ll, 1, 0).wait_send()
            gather_y(k, y, ll, -1, 1).wait_send()
            gather_y(k, y, ll, 1, 2).wait_send()
            send_hop1(k, ll, 1).wait_send()
            send_hop2(k, ll, 1).wait_send()
            send_hop2(k, ll, -1).wait_send()

            @pl.when(ahead != 0)
            def _():
                send_ring(k, ll, 1).wait_send()

        return carry

    lax.fori_loop(0, 8, settle, 0)


def shards(section_inputs, loss_grads, weight_codes, proj_weight):
    codes = jnp.broadcast_to(weight_codes.astype(F32)[:, :, None], (2, TOK, 128))
    anywhere = pl.BlockSpec(memory_space=pl.ANY)
    vmem = pl.BlockSpec(memory_space=pltpu.VMEM)
    dma = pltpu.SemaphoreType.DMA
    blocks = (2, 8, ROWS, HIDDEN)
    return pl.pallas_call(
        kernel,
        out_shape=jax.ShapeDtypeStruct((1, ROWS, HIDDEN), F32),
        in_specs=[anywhere, anywhere, vmem, vmem],
        out_specs=vmem,
        scratch_shapes=[
            pltpu.VMEM((2, 32, ROWS, HIDDEN), BF16),
            pltpu.VMEM((2, TOK, WIDTH), BF16),
            pltpu.VMEM((2, TOK, WIDTH), BF16),
            pltpu.VMEM((2, CHUNKS, TOK, COLS), BF16),
            pltpu.VMEM((CHUNKS, TOK, COLS), BF16),
            pltpu.VMEM((2, 2 * TOK, HIDDEN), BF16),
            pltpu.VMEM((2, TOK, HIDDEN), F32),
            pltpu.VMEM((2, TOK, HIDDEN), F32),
            pltpu.VMEM((2, TOK, 128), F32),
            pltpu.VMEM((2, 32, ROWS, HIDDEN), BF16),
            pltpu.VMEM(blocks, BF16),
            pltpu.VMEM(blocks, BF16),
            pltpu.VMEM(blocks, BF16),
            pltpu.VMEM(blocks, BF16),
            pltpu.VMEM(blocks, BF16),
            pltpu.VMEM((2, ROWS, HIDDEN), F32),
            pltpu.VMEM((6, 8, 128), F32),
            pltpu.VMEM((5, 8, 128), F32),
            pltpu.VMEM((TOK, WIDTH), BF16),
            dma((3,)),
            dma((2, 32)),
            dma((2, 2, 8)),
            dma((3, 2, 8)),
            dma((3,)),
            dma((2,)),
            dma((CHUNKS,)),
            dma((CHUNKS,)),
            dma((2, 8)),
            dma((2, 8)),
            dma((2, 8)),
            dma((2, 8)),
            dma((2, 8)),
            dma((3, 2, 8)),
            dma((2, 8)),
            dma((1,)),
            dma((1,)),
            dma((5,)),
            dma((5,)),
        ],
        compiler_params=pltpu.CompilerParams(
            collective_id=0, has_side_effects=True, vmem_limit_bytes=56 * 2**20
        ),
    )(section_inputs[0][None], loss_grads, codes, proj_weight)


def solution(mesh):
    return jax.shard_map(
        shards,
        mesh=mesh,
        in_specs=(
            P("section", None, "dp", None),
            P(None, "dp", None),
            P(None, "dp"),
            P("section", "dp", None),
        ),
        out_specs=P("section", "dp", None),
        check_vma=False,
    )
```

```python
import jax
import jax.numpy as jnp
from jax import lax
from jax.experimental import pallas as pl
from jax.experimental.pallas import tpu as pltpu
from jax.sharding import PartitionSpec as P

MESH = pl.DeviceIdType.MESH
F32 = jnp.float32
BF16 = jnp.bfloat16
EPSILON = 1e-06
TOK = 64
WIDTH = 4096
HIDDEN = 512
ROWS = 128
CHUNKS = 8
COLS = WIDTH // CHUNKS
GROUPS = COLS // ROWS


def device(x, z, core, y):
    return (x * 4 + (z // 8) * 2 + core, y * 8 + z % 8)


def kernel(
    inputs, loss, codes, shard, out,
    weights, units, normed, grads, outgoing, factors, project, slope, inv_rms, partial,
    hop1, hop2p, hop2m, ringp, ringm, final, tally, staged,
    local_sem, gather_recv, gather_z_send, gather_y_send, cross_send, cross_recv,
    chain_send, chain_recv, hop1_recv, hop2p_recv, hop2m_recv, ringp_recv, ringm_recv,
    sum_y_send, sum_z_send, final_send, final_recv, tally_send, tally_recv,
):
    section = lax.axis_index("section")
    group = lax.axis_index("dp")
    x, half, core = section // 4, (section // 2) % 2, section % 2
    y, low = group // 8, group % 8
    z = half * 8 + low
    sister = device(x, z, 1 - core, y)
    zdev = {s: device(x, (z + 16 + s) % 16, core, y) for s in (1, -1)}
    ydev = {s: device(x, z, core, (y + 4 + s) % 4) for s in (1, -1)}
    home = core == half
    first = jnp.logical_and(x == 3, core == 1)
    last = jnp.logical_and(x == 0, core == 0)
    far = (z + 8) % 16
    next_x = device((x + 3) % 4, z, 1, y)
    prev_x = device((x + 1) % 4, z, 0, y)

    barrier = pltpu.get_barrier_semaphore()

    def greet(target):
        pl.semaphore_signal(barrier, inc=1, device_id=target, device_id_type=MESH)

    for s in (1, -1):
        greet(zdev[s])
        greet(ydev[s])
    greet(sister)

    @pl.when(jnp.logical_not(home))
    def _():
        greet(device(x, far, 0, y))
        greet(device(x, far, 1, y))

    @pl.when(jnp.logical_and(core == 1, x < 3))
    def _():
        greet(prev_x)

    pl.semaphore_wait(barrier, 6 + (1 - core) * ((x + 3) // 4))

    def remote(src, dst, send, recv, target):
        return pltpu.make_async_remote_copy(
            src_ref=src, dst_ref=dst, send_sem=send, recv_sem=recv,
            device_id=target, device_id_type=MESH,
        )

    here = y * 8 + low

    def own_weight():
        return pltpu.make_async_copy(shard.at[0], weights.at[core, here], local_sem.at[0])

    def lend_weight():
        return remote(
            shard.at[0], weights.at[core, here], cross_send.at[0],
            gather_recv.at[core, here], sister,
        )

    def own_inputs():
        return pltpu.make_async_copy(inputs.at[0, half], units.at[core], local_sem.at[1])

    def lend_inputs():
        return remote(
            inputs.at[0, half], units.at[core], cross_send.at[1], cross_recv.at[core], sister
        )

    def cross_inputs(first_row, rows):
        part = pl.ds(first_row, rows)
        return remote(
            inputs.at[0, 1 - half, part], units.at[core, part], cross_send.at[2],
            cross_recv.at[core], device(x, far, half, y),
        )

    def seed_copy():
        return pltpu.make_async_copy(loss.at[half], staged, local_sem.at[2])

    @pl.when(home)
    def _():
        own_weight().start()
        own_inputs().start()

    @pl.when(jnp.logical_not(home))
    def _():
        lend_weight().start()
        lend_inputs().start()

    seed_copy().start()

    def block_ref(k, yy, ll):
        return weights.at[k, yy * 8 + ll]

    def gather_z(k, ll, sgn):
        return remote(
            block_ref(k, y, ll), block_ref(k, y, ll), gather_z_send.at[(1 - sgn) // 2, k, ll],
            gather_recv.at[k, y * 8 + ll], zdev[sgn],
        )

    def gather_y(k, yy, ll, sgn, slot):
        return remote(
            block_ref(k, yy, ll), block_ref(k, yy, ll), gather_y_send.at[slot, k, ll],
            gather_recv.at[k, yy * 8 + ll], ydev[sgn],
        )

    def arrived(k, yy, ll):
        remote(
            block_ref(k, yy, ll), block_ref(k, yy, ll), cross_send.at[0],
            gather_recv.at[k, yy * 8 + ll], sister,
        ).wait_recv()

    def side(ll):
        return 1 - 2 * (ll % 2)

    def ring_place(t, sgn):
        zz = (z + 16 - sgn * t) % 16
        return zz // 8 == core, zz % 8

    def spread_y(k, ll):
        gather_y(k, y, ll, 1, 0).start()
        gather_y(k, y, ll, -1, 1).start()

    @pl.when(home)
    def _():
        own_weight().wait()

        def begin(k):
            for sgn in (1, -1):
                gather_z(k, low, sgn).start()
            spread_y(k, low)

        begin(core)
        arrived(1 - core, y, low)
        begin(1 - core)

    def relay_y(t, sgn):
        valid, ll = ring_place(t, sgn)
        valid = jnp.logical_and(valid, jnp.logical_or(t < 8, side(ll) == sgn))

        @pl.when(valid)
        def _():
            for k in (1, 0):
                arrived(k, (y + 3) % 4, ll)

                @pl.when(side(ll) == 1)
                def _():
                    gather_y(k, (y + 3) % 4, ll, 1, 2).start()

                arrived(k, (y + 1) % 4, ll)

                @pl.when(side(ll) == -1)
                def _():
                    gather_y(k, (y + 1) % 4, ll, -1, 2).start()

    def relay_z(t, sgn):
        valid, ll = ring_place(t, sgn)
        valid = jnp.logical_and(valid, jnp.logical_or(t < 8, side(ll) == sgn))
        onward = jnp.logical_or(t < 7, jnp.logical_and(t == 7, side(ll) == sgn))

        @pl.when(valid)
        def _():
            for k in (1, 0):
                arrived(k, y, ll)

                @pl.when(onward)
                def _():
                    gather_z(k, ll, sgn).start()

                spread_y(k, ll)

    def pass_tally(slot, target):
        return remote(
            tally.at[slot], tally.at[slot + 1], tally_send.at[slot], tally_recv.at[slot + 1],
            target,
        )

    tally[0] = jnp.broadcast_to(
        jnp.sum(codes[0] + codes[1], axis=0, keepdims=True), (8, 128)
    )
    pass_tally(0, zdev[1]).start()

    def tally_y(slot):
        pass_tally(slot - 1, ydev[1]).wait_recv()
        pass_tally(slot, ydev[1]).start()

    def gather_step(t, carry):
        @pl.when(t % 2 == 1)
        def _():
            cross_inputs(((t - 1) // 2) * (TOK // 4), TOK // 4).start()

        for sgn in (1, -1):
            relay_z(t, sgn)

        @pl.when(t == 1)
        def _():
            relay_y(0, 1)

        @pl.when(t > 1)
        def _():
            for sgn in (1, -1):
                relay_y(t - 1, sgn)

        @pl.when(t < 7)
        def _():
            pass_tally(t - 1, zdev[1]).wait_recv()
            pass_tally(t, zdev[1]).start()

        return carry

    lax.fori_loop(1, 9, gather_step, 0)
    for sgn in (1, -1):
        relay_y(8, sgn)

    pass_tally(6, zdev[1]).wait_recv()
    tally[8] = sum(tally[i] for i in range(1, 8)) + tally[0]
    pass_tally(8, ydev[1]).start()

    seed_copy().wait()

    @pl.when(first)
    def _():
        scale = codes[half, :, 0:1] / 127.0
        for j in range(CHUNKS):
            part = staged[:, j * COLS:(j + 1) * COLS].astype(F32)
            grads[1, j] = (part * scale).astype(BF16)

    @pl.when(home)
    def _():
        own_inputs().wait()

    def inputs_arrived(k):
        remote(
            units.at[k], units.at[k], cross_send.at[1], cross_recv.at[k], sister
        ).wait_recv()

    @pl.when(home)
    def _():
        inputs_arrived(1 - core)

    @pl.when(jnp.logical_not(home))
    def _():
        inputs_arrived(0)
        inputs_arrived(1)

    def far_arrived(ll, carry):
        for k in (1, 0):
            arrived(k, (y + 2) % 4, ll)
        return carry

    lax.fori_loop(0, 8, far_arrived, 0)

    def weight_chunk(k, j):
        return weights[k, j * GROUPS:(j + 1) * GROUPS].reshape(COLS, HIDDEN)

    def columns(ref, k, j):
        return ref[k, :, j * COLS:(j + 1) * COLS]

    def unrolled(body, carry):
        for j in range(CHUNKS):
            carry = body(j, carry)
        return carry

    def prepare(k):
        def square(j, acc):
            v = columns(units, k, j).astype(F32)
            return acc + jnp.sum(v * v, axis=-1, keepdims=True)

        total = unrolled(square, jnp.zeros((TOK, 1), F32))
        inv = lax.rsqrt(total / WIDTH + EPSILON)
        inv_rms[k] = jnp.broadcast_to(inv, (TOK, 128))

        def multiply(j, acc):
            row = (columns(units, k, j).astype(F32) * inv).astype(BF16)
            normed[k, :, j * COLS:(j + 1) * COLS] = row
            return acc + jnp.dot(row, weight_chunk(k, j), preferred_element_type=F32)

        value = unrolled(multiply, jnp.zeros((TOK, HIDDEN), F32))
        prob = jax.nn.sigmoid(value)
        project[k] = value
        slope[k] = prob * (1.0 + value * (1.0 - prob))
        factors[k, TOK:] = (value * prob).astype(BF16)

    for k in (1, 0):
        prepare(k)

    def chain(j, target):
        return remote(outgoing.at[j], grads.at[1, j], chain_send.at[j], chain_recv.at[j], target)

    def stage(k):
        def act_grad(j, acc):
            if k == 1:
                @pl.when(jnp.logical_not(first))
                def _():
                    chain(j, sister).wait_recv()
            return acc + jnp.dot(grads[k, j], weight_chunk(k, j), preferred_element_type=F32)

        grad_act = unrolled(act_grad, jnp.zeros((TOK, HIDDEN), F32))
        grad_proj = (grad_act * slope[k]).astype(BF16)
        factors[k, :TOK] = grad_proj
        mean = jnp.sum(grad_proj.astype(F32) * project[k], axis=-1, keepdims=True) / WIDTH
        inv = inv_rms[k, :, 0:1]

        def in_grad(j, carry):
            norm = lax.dot_general(
                grad_proj, weight_chunk(k, j), (((1,), (1,)), ((), ())),
                preferred_element_type=F32,
            )
            unit = columns(units, k, j).astype(F32) * inv
            result = (grads[k, j].astype(F32) + inv * (norm - unit * mean)).astype(BF16)
            if k == 1:
                grads[0, j] = result
            else:
                outgoing[j] = result

                @pl.when(core == 1)
                def _():
                    chain(j, sister).start()

                @pl.when(core == 0)
                def _():
                    chain(j, next_x).start()

            return carry

        def onward():
            unrolled(in_grad, 0)

        if k == 1:
            onward()
        else:
            pl.when(jnp.logical_not(last))(onward)

    stage(1)
    tally_y(9)
    stage(0)
    tally_y(10)

    def weight_grad(k):
        def rows(j, carry):
            left = jnp.concatenate([columns(normed, k, j), grads[k, j]], axis=0)
            term = lax.dot_general(
                left, factors[k], (((0,), (0,)), ((), ())), preferred_element_type=F32
            )
            partial[k, j * GROUPS:(j + 1) * GROUPS] = term.astype(BF16).reshape(
                GROUPS, ROWS, HIDDEN
            )
            return carry

        unrolled(rows, 0)

    def part_ref(k, dy, ll):
        return partial.at[k, ((y + 4 + dy) % 4) * 8 + ll]

    def send_hop1(k, ll, sgn):
        return remote(
            part_ref(k, 2, ll), hop1.at[k, ll], sum_y_send.at[0, k, ll], hop1_recv.at[k, ll],
            ydev[sgn],
        )

    def send_hop2(k, ll, sgn):
        land, sem = (hop2p, hop2p_recv) if sgn == 1 else (hop2m, hop2m_recv)
        return remote(
            part_ref(k, sgn, ll), land.at[k, ll], sum_y_send.at[(3 - sgn) // 2, k, ll],
            sem.at[k, ll], ydev[sgn],
        )

    def send_ring(k, ll, sgn):
        land, sem = (ringp, ringp_recv) if sgn == 1 else (ringm, ringm_recv)
        return remote(
            part_ref(k, 0, ll), land.at[k, ll], sum_z_send.at[k, ll], sem.at[k, ll], zdev[sgn]
        )

    def target_place(t, sgn):
        zz = (z + 16 + sgn * t) % 16
        ll = zz % 8
        valid = jnp.logical_and(zz // 8 == core, jnp.logical_or(t < 8, side(ll) == sgn))
        return valid, ll

    def begin_y(k, t, sgn):
        valid, ll = target_place(t, sgn)

        @pl.when(valid)
        def _():
            @pl.when(side(ll) == 1)
            def _():
                send_hop1(k, ll, 1).start()
                send_hop2(k, ll, -1).start()

            @pl.when(side(ll) == -1)
            def _():
                send_hop1(k, ll, -1).start()
                send_hop2(k, ll, 1).start()

    def begin_sum(k):
        def body(i, carry):
            for sgn in (1, -1):
                begin_y(k, 8 - i, sgn)
            return carry

        lax.fori_loop(0, 8, body, 0)
        begin_y(k, 0, 1)

    def add_into(k, dy, ll, extra):
        index = ((y + 4 + dy) % 4) * 8 + ll
        value = partial[k, index].astype(F32)
        for ref in extra:
            value = value + ref[k, ll].astype(F32)
        partial[k, index] = value.astype(BF16)

    def middle_y(t, sgn):
        valid, ll = target_place(t, sgn)

        @pl.when(valid)
        def _():
            for k in (1, 0):
                send_hop1(k, ll, 1).wait_recv()

                @pl.when(side(ll) == 1)
                def _():
                    add_into(k, 1, ll, (hop1,))
                    send_hop2(k, ll, 1).start()

                @pl.when(side(ll) == -1)
                def _():
                    add_into(k, -1, ll, (hop1,))
                    send_hop2(k, ll, -1).start()

    def ring_sum(t, sgn):
        valid, ll = target_place(t, sgn)
        fed = jnp.logical_or(t < 7, jnp.logical_and(t == 7, side(ll) == sgn))
        land = ringp if sgn == 1 else ringm

        @pl.when(valid)
        def _():
            for k in (1, 0):
                send_hop2(k, ll, 1).wait_recv()
                send_hop2(k, ll, -1).wait_recv()

                @pl.when(fed)
                def _():
                    send_ring(k, ll, sgn).wait_recv()
                    add_into(k, 0, ll, (hop2p, hop2m, land))

                @pl.when(jnp.logical_not(fed))
                def _():
                    add_into(k, 0, ll, (hop2p, hop2m))

                send_ring(k, ll, sgn).start()

    for k in (1, 0):
        weight_grad(k)
        begin_sum(k)

    def sum_step(i, carry):
        @pl.when(i < 8)
        def _():
            for sgn in (1, -1):
                middle_y(8 - i, sgn)

        @pl.when(i == 8)
        def _():
            middle_y(0, 1)

        @pl.when(jnp.logical_and(i >= 1, i < 9))
        def _():
            for sgn in (1, -1):
                ring_sum(9 - i, sgn)

        return carry

    lax.fori_loop(0, 9, sum_step, 0)

    pass_tally(10, ydev[1]).wait_recv()
    scale = 127.0 / sum(tally[i] for i in range(8, 12))[0:1, 0:1]

    def send_final():
        return remote(final.at[0], final.at[1], final_send.at[0], final_recv.at[0], sister)

    @pl.when(home)
    def _():
        def total(k):
            for sgn in (1, -1):
                send_hop2(k, low, sgn).wait_recv()
                send_ring(k, low, sgn).wait_recv()
            value = partial[k, here].astype(F32)
            for ref in (hop2p, hop2m, ringp, ringm):
                value = value + ref[k, low].astype(F32)
            return value

        final[0] = total(1 - core)
        send_final().start()
        out[0] = total(core) * scale
        send_final().wait_send()

    @pl.when(jnp.logical_not(home))
    def _():
        send_final().wait_recv()
        out[0] = final[1] * scale

    @pl.when(jnp.logical_not(home))
    def _():
        lend_weight().wait_send()
        lend_inputs().wait_send()

    cross_inputs(0, TOK).wait_send()

    @pl.when(jnp.logical_not(last))
    def _():
        for j in range(CHUNKS):
            chain(j, sister).wait_send()

    for i in (0, 1, 2, 3, 4, 5, 6, 8, 9, 10):
        pass_tally(i, sister).wait_send()

    def settle(ll, carry):
        zz = core * 8 + ll
        ahead = (z + 16 - zz) % 16
        plus = jnp.logical_or(ahead < 7, jnp.logical_and(ahead == 7, side(ll) == 1))
        back = (16 - ahead) % 16
        minus = jnp.logical_or(back < 7, jnp.logical_and(back == 7, side(ll) == -1))
        for k in (1, 0):
            @pl.when(plus)
            def _():
                gather_z(k, ll, 1).wait_send()

            @pl.when(minus)
            def _():
                gather_z(k, ll, -1).wait_send()

            gather_y(k, y, ll, 1, 0).wait_send()
            gather_y(k, y, ll, -1, 1).wait_send()
            gather_y(k, y, ll, 1, 2).wait_send()
            send_hop1(k, ll, 1).wait_send()
            send_hop2(k, ll, 1).wait_send()
            send_hop2(k, ll, -1).wait_send()

            @pl.when(ahead != 0)
            def _():
                send_ring(k, ll, 1).wait_send()

        return carry

    lax.fori_loop(0, 8, settle, 0)


def shards(section_inputs, loss_grads, weight_codes, proj_weight):
    codes = jnp.broadcast_to(weight_codes.astype(F32)[:, :, None], (2, TOK, 128))
    anywhere = pl.BlockSpec(memory_space=pl.ANY)
    vmem = pl.BlockSpec(memory_space=pltpu.VMEM)
    dma = pltpu.SemaphoreType.DMA
    blocks = (2, 8, ROWS, HIDDEN)
    return pl.pallas_call(
        kernel,
        out_shape=jax.ShapeDtypeStruct((1, ROWS, HIDDEN), F32),
        in_specs=[anywhere, anywhere, vmem, vmem],
        out_specs=vmem,
        scratch_shapes=[
            pltpu.VMEM((2, 32, ROWS, HIDDEN), BF16),
            pltpu.VMEM((2, TOK, WIDTH), BF16),
            pltpu.VMEM((2, TOK, WIDTH), BF16),
            pltpu.VMEM((2, CHUNKS, TOK, COLS), BF16),
            pltpu.VMEM((CHUNKS, TOK, COLS), BF16),
            pltpu.VMEM((2, 2 * TOK, HIDDEN), BF16),
            pltpu.VMEM((2, TOK, HIDDEN), F32),
            pltpu.VMEM((2, TOK, HIDDEN), F32),
            pltpu.VMEM((2, TOK, 128), F32),
            pltpu.VMEM((2, 32, ROWS, HIDDEN), BF16),
            pltpu.VMEM(blocks, BF16),
            pltpu.VMEM(blocks, BF16),
            pltpu.VMEM(blocks, BF16),
            pltpu.VMEM(blocks, BF16),
            pltpu.VMEM(blocks, BF16),
            pltpu.VMEM((2, ROWS, HIDDEN), F32),
            pltpu.VMEM((12, 8, 128), F32),
            pltpu.VMEM((TOK, WIDTH), BF16),
            dma((3,)),
            dma((2, 32)),
            dma((2, 2, 8)),
            dma((3, 2, 8)),
            dma((3,)),
            dma((2,)),
            dma((CHUNKS,)),
            dma((CHUNKS,)),
            dma((2, 8)),
            dma((2, 8)),
            dma((2, 8)),
            dma((2, 8)),
            dma((2, 8)),
            dma((3, 2, 8)),
            dma((2, 8)),
            dma((1,)),
            dma((1,)),
            dma((12,)),
            dma((12,)),
        ],
        compiler_params=pltpu.CompilerParams(
            collective_id=0, has_side_effects=True, vmem_limit_bytes=56 * 2**20
        ),
    )(section_inputs[0][None], loss_grads, codes, proj_weight)


def solution(mesh):
    return jax.shard_map(
        shards,
        mesh=mesh,
        in_specs=(
            P("section", None, "dp", None),
            P(None, "dp", None),
            P(None, "dp"),
            P("section", "dp", None),
        ),
        out_specs=P("section", "dp", None),
        check_vma=False,
    )
```

```python
import jax
import jax.numpy as jnp
from jax import lax
from jax.experimental import pallas as pl
from jax.experimental.pallas import tpu as pltpu
from jax.sharding import PartitionSpec as P

MESH = pl.DeviceIdType.MESH
F32 = jnp.float32
BF16 = jnp.bfloat16
EPSILON = 1e-06
TOK = 64
WIDTH = 4096
HIDDEN = 512
ROWS = 128
CHUNKS = 8
COLS = WIDTH // CHUNKS
GROUPS = COLS // ROWS
SPLIT = 384
REST = HIDDEN - SPLIT
AHEAD = 1


def device(x, z, core, y):
    return (x * 4 + (z // 8) * 2 + core, y * 8 + z % 8)


def kernel(
    inputs, loss, codes, shard, out,
    weights, units, normed, grads, outgoing, factors, project, slope, inv_rms, partial, wide,
    hop1, hop2p, hop2m, ringp, ringm, widep, widem, end1, end2p, end2m, final, tally, staged,
    local_sem, gather_recv, gather_z_send, gather_y_send, cross_send, cross_recv,
    chain_send, chain_recv, hop1_recv, hop2p_recv, hop2m_recv, ringp_recv, ringm_recv,
    widep_recv, widem_recv, end1_recv, end2p_recv, end2m_recv, wide_send, end_send,
    sum_y_send, sum_z_send, final_send, final_recv, tally_send, tally_recv,
):
    section = lax.axis_index("section")
    group = lax.axis_index("dp")
    x, half, core = section // 4, (section // 2) % 2, section % 2
    y, low = group // 8, group % 8
    z = half * 8 + low
    sister = device(x, z, 1 - core, y)
    zdev = {s: device(x, (z + 16 + s) % 16, core, y) for s in (1, -1)}
    ydev = {s: device(x, z, core, (y + 4 + s) % 4) for s in (1, -1)}
    home = core == half
    first = jnp.logical_and(x == 3, core == 1)
    last = jnp.logical_and(x == 0, core == 0)
    far = (z + 8) % 16
    next_x = device((x + 3) % 4, z, 1, y)
    prev_x = device((x + 1) % 4, z, 0, y)

    barrier = pltpu.get_barrier_semaphore()

    def greet(target):
        pl.semaphore_signal(barrier, inc=1, device_id=target, device_id_type=MESH)

    for s in (1, -1):
        greet(zdev[s])
        greet(ydev[s])
    greet(sister)

    @pl.when(jnp.logical_not(home))
    def _():
        greet(device(x, far, 0, y))
        greet(device(x, far, 1, y))

    @pl.when(jnp.logical_and(core == 1, x < 3))
    def _():
        greet(prev_x)

    pl.semaphore_wait(barrier, 6 + (1 - core) * ((x + 3) // 4))

    def remote(src, dst, send, recv, target):
        return pltpu.make_async_remote_copy(
            src_ref=src, dst_ref=dst, send_sem=send, recv_sem=recv,
            device_id=target, device_id_type=MESH,
        )

    here = y * 8 + low

    def own_weight():
        return pltpu.make_async_copy(shard.at[0], weights.at[core, here], local_sem.at[0])

    def lend_weight():
        return remote(
            shard.at[0], weights.at[core, here], cross_send.at[0],
            gather_recv.at[core, here], sister,
        )

    def own_inputs():
        return pltpu.make_async_copy(inputs.at[0, half], units.at[core], local_sem.at[1])

    def lend_inputs():
        return remote(
            inputs.at[0, half], units.at[core], cross_send.at[1], cross_recv.at[core], sister
        )

    def cross_inputs(first_row, rows):
        part = pl.ds(first_row, rows)
        return remote(
            inputs.at[0, 1 - half, part], units.at[core, part], cross_send.at[2],
            cross_recv.at[core], device(x, far, half, y),
        )

    def seed_copy():
        return pltpu.make_async_copy(loss.at[half], staged, local_sem.at[2])

    @pl.when(home)
    def _():
        own_weight().start()
        own_inputs().start()

    @pl.when(jnp.logical_not(home))
    def _():
        lend_weight().start()
        lend_inputs().start()

    seed_copy().start()

    def block_ref(k, yy, ll):
        return weights.at[k, yy * 8 + ll]

    def gather_z(k, ll, sgn):
        return remote(
            block_ref(k, y, ll), block_ref(k, y, ll), gather_z_send.at[(1 - sgn) // 2, k, ll],
            gather_recv.at[k, y * 8 + ll], zdev[sgn],
        )

    def gather_y(k, yy, ll, sgn, slot):
        return remote(
            block_ref(k, yy, ll), block_ref(k, yy, ll), gather_y_send.at[slot, k, ll],
            gather_recv.at[k, yy * 8 + ll], ydev[sgn],
        )

    def arrived(k, yy, ll):
        remote(
            block_ref(k, yy, ll), block_ref(k, yy, ll), cross_send.at[0],
            gather_recv.at[k, yy * 8 + ll], sister,
        ).wait_recv()

    def side(ll):
        return 1 - 2 * (ll % 2)

    def ring_place(t, sgn):
        zz = (z + 16 - sgn * t) % 16
        return zz // 8 == core, zz % 8

    def spread_y(k, ll):
        gather_y(k, y, ll, 1, 0).start()
        gather_y(k, y, ll, -1, 1).start()

    @pl.when(home)
    def _():
        own_weight().wait()

        def begin(k):
            for sgn in (1, -1):
                gather_z(k, low, sgn).start()
            spread_y(k, low)

        begin(core)
        arrived(1 - core, y, low)
        begin(1 - core)

    def relay_y(t, sgn):
        valid, ll = ring_place(t, sgn)
        valid = jnp.logical_and(valid, jnp.logical_or(t < 8, side(ll) == sgn))

        @pl.when(valid)
        def _():
            for k in (1, 0):
                arrived(k, (y + 3) % 4, ll)

                @pl.when(side(ll) == 1)
                def _():
                    gather_y(k, (y + 3) % 4, ll, 1, 2).start()

                arrived(k, (y + 1) % 4, ll)

                @pl.when(side(ll) == -1)
                def _():
                    gather_y(k, (y + 1) % 4, ll, -1, 2).start()

    def relay_z(t, sgn):
        valid, ll = ring_place(t, sgn)
        valid = jnp.logical_and(valid, jnp.logical_or(t < 8, side(ll) == sgn))
        onward = jnp.logical_or(t < 7, jnp.logical_and(t == 7, side(ll) == sgn))

        @pl.when(valid)
        def _():
            for k in (1, 0):
                arrived(k, y, ll)

                @pl.when(onward)
                def _():
                    gather_z(k, ll, sgn).start()

                spread_y(k, ll)

    def pass_tally(slot, target):
        return remote(
            tally.at[slot], tally.at[slot + 1], tally_send.at[slot], tally_recv.at[slot + 1],
            target,
        )

    tally[0] = jnp.broadcast_to(
        jnp.sum(codes[0] + codes[1], axis=0, keepdims=True), (8, 128)
    )
    pass_tally(0, zdev[1]).start()

    def tally_y(slot):
        pass_tally(slot - 1, ydev[1]).wait_recv()
        pass_tally(slot, ydev[1]).start()

    def gather_step(t, carry):
        @pl.when(t % 2 == 1)
        def _():
            cross_inputs(((t - 1) // 2) * (TOK // 4), TOK // 4).start()

        for sgn in (1, -1):
            relay_z(t, sgn)

        @pl.when(t == 1)
        def _():
            relay_y(0, 1)

        @pl.when(t > 1)
        def _():
            for sgn in (1, -1):
                relay_y(t - 1, sgn)

        @pl.when(t < 7)
        def _():
            pass_tally(t - 1, zdev[1]).wait_recv()
            pass_tally(t, zdev[1]).start()

        return carry

    lax.fori_loop(1, 9, gather_step, 0)
    for sgn in (1, -1):
        relay_y(8, sgn)

    pass_tally(6, zdev[1]).wait_recv()
    tally[8] = sum(tally[i] for i in range(1, 8)) + tally[0]
    pass_tally(8, ydev[1]).start()

    seed_copy().wait()

    @pl.when(first)
    def _():
        scale = codes[half, :, 0:1] / 127.0
        for j in range(CHUNKS):
            part = staged[:, j * COLS:(j + 1) * COLS].astype(F32)
            grads[1, j] = (part * scale).astype(BF16)

    @pl.when(home)
    def _():
        own_inputs().wait()

    def inputs_arrived(k):
        remote(
            units.at[k], units.at[k], cross_send.at[1], cross_recv.at[k], sister
        ).wait_recv()

    @pl.when(home)
    def _():
        inputs_arrived(1 - core)

    @pl.when(jnp.logical_not(home))
    def _():
        inputs_arrived(0)
        inputs_arrived(1)

    def far_arrived(ll, carry):
        for k in (1, 0):
            arrived(k, (y + 2) % 4, ll)
        return carry

    lax.fori_loop(0, 8, far_arrived, 0)

    def weight_chunk(k, j):
        return weights[k, j * GROUPS:(j + 1) * GROUPS].reshape(COLS, HIDDEN)

    def columns(ref, k, j):
        return ref[k, :, j * COLS:(j + 1) * COLS]

    def unrolled(body, carry):
        for j in range(CHUNKS):
            carry = body(j, carry)
        return carry

    def prepare(k):
        def square(j, acc):
            v = columns(units, k, j).astype(F32)
            return acc + jnp.sum(v * v, axis=-1, keepdims=True)

        total = unrolled(square, jnp.zeros((TOK, 1), F32))
        inv = lax.rsqrt(total / WIDTH + EPSILON)
        inv_rms[k] = jnp.broadcast_to(inv, (TOK, 128))

        def multiply(j, acc):
            row = (columns(units, k, j).astype(F32) * inv).astype(BF16)
            normed[k, :, j * COLS:(j + 1) * COLS] = row
            return acc + jnp.dot(row, weight_chunk(k, j), preferred_element_type=F32)

        value = unrolled(multiply, jnp.zeros((TOK, HIDDEN), F32))
        prob = jax.nn.sigmoid(value)
        project[k] = value
        slope[k] = prob * (1.0 + value * (1.0 - prob))
        factors[k, TOK:] = (value * prob).astype(BF16)

    for k in (1, 0):
        prepare(k)

    def chain(j, target):
        return remote(outgoing.at[j], grads.at[1, j], chain_send.at[j], chain_recv.at[j], target)

    def stage(k):
        def act_grad(j, acc):
            if k == 1:
                @pl.when(jnp.logical_not(first))
                def _():
                    chain(j, sister).wait_recv()
            return acc + jnp.dot(grads[k, j], weight_chunk(k, j), preferred_element_type=F32)

        grad_act = unrolled(act_grad, jnp.zeros((TOK, HIDDEN), F32))
        grad_proj = (grad_act * slope[k]).astype(BF16)
        factors[k, :TOK] = grad_proj
        mean = jnp.sum(grad_proj.astype(F32) * project[k], axis=-1, keepdims=True) / WIDTH
        inv = inv_rms[k, :, 0:1]

        def in_grad(j, carry):
            norm = lax.dot_general(
                grad_proj, weight_chunk(k, j), (((1,), (1,)), ((), ())),
                preferred_element_type=F32,
            )
            unit = columns(units, k, j).astype(F32) * inv
            result = (grads[k, j].astype(F32) + inv * (norm - unit * mean)).astype(BF16)
            if k == 1:
                grads[0, j] = result
            else:
                outgoing[j] = result

                @pl.when(core == 1)
                def _():
                    chain(j, sister).start()

                @pl.when(core == 0)
                def _():
                    chain(j, next_x).start()

            return carry

        def onward():
            unrolled(in_grad, 0)

        if k == 1:
            onward()
        else:
            pl.when(jnp.logical_not(last))(onward)

    stage(1)
    tally_y(9)
    stage(0)
    tally_y(10)

    def weight_grad(k):
        def rows(j, carry):
            left = jnp.concatenate([columns(normed, k, j), grads[k, j]], axis=0)
            term = lax.dot_general(
                left, factors[k], (((0,), (0,)), ((), ())), preferred_element_type=F32
            )
            term = term.astype(BF16)
            for i in range(GROUPS):
                place = j * GROUPS + i
                block = term[i * ROWS:(i + 1) * ROWS]
                partial[k, place] = block[:, :SPLIT]
                wide[k, place % 8, place // 8] = block[:, SPLIT:]
            return carry

        unrolled(rows, 0)

    def part_ref(k, dy, ll):
        return partial.at[k, ((y + 4 + dy) % 4) * 8 + ll]

    def send_hop1(k, ll, sgn):
        return remote(
            part_ref(k, 2, ll), hop1.at[k, ll], sum_y_send.at[0, k, ll], hop1_recv.at[k, ll],
            ydev[sgn],
        )

    def send_hop2(k, ll, sgn):
        land, sem = (hop2p, hop2p_recv) if sgn == 1 else (hop2m, hop2m_recv)
        return remote(
            part_ref(k, sgn, ll), land.at[k, ll], sum_y_send.at[(3 - sgn) // 2, k, ll],
            sem.at[k, ll], ydev[sgn],
        )

    def send_ring(k, ll, sgn):
        land, sem = (ringp, ringp_recv) if sgn == 1 else (ringm, ringm_recv)
        return remote(
            part_ref(k, 0, ll), land.at[k, ll], sum_z_send.at[k, ll], sem.at[k, ll], zdev[sgn]
        )

    def target_place(t, sgn):
        zz = (z + 16 + sgn * t) % 16
        ll = zz % 8
        valid = jnp.logical_and(zz // 8 == core, jnp.logical_or(t < 8, side(ll) == sgn))
        return valid, ll

    def begin_y(k, t, sgn):
        valid, ll = target_place(t, sgn)

        @pl.when(valid)
        def _():
            @pl.when(side(ll) == 1)
            def _():
                send_hop1(k, ll, 1).start()
                send_hop2(k, ll, -1).start()

            @pl.when(side(ll) == -1)
            def _():
                send_hop1(k, ll, -1).start()
                send_hop2(k, ll, 1).start()

    def begin_sum(k):
        def body(i, carry):
            for sgn in (1, -1):
                begin_y(k, 8 - i, sgn)
            return carry

        lax.fori_loop(0, AHEAD, body, 0)

    def add_into(k, dy, ll, extra):
        index = ((y + 4 + dy) % 4) * 8 + ll
        value = partial[k, index].astype(F32)
        for ref in extra:
            value = value + ref[k, ll].astype(F32)
        partial[k, index] = value.astype(BF16)

    def middle_y(t, sgn):
        valid, ll = target_place(t, sgn)

        @pl.when(valid)
        def _():
            for k in (1, 0):
                send_hop1(k, ll, 1).wait_recv()

                @pl.when(side(ll) == 1)
                def _():
                    add_into(k, 1, ll, (hop1,))
                    send_hop2(k, ll, 1).start()

                @pl.when(side(ll) == -1)
                def _():
                    add_into(k, -1, ll, (hop1,))
                    send_hop2(k, ll, -1).start()

    def ring_sum(t, sgn):
        valid, ll = target_place(t, sgn)
        fed = jnp.logical_or(t < 7, jnp.logical_and(t == 7, side(ll) == sgn))
        land = ringp if sgn == 1 else ringm

        @pl.when(valid)
        def _():
            for k in (1, 0):
                send_hop2(k, ll, 1).wait_recv()
                send_hop2(k, ll, -1).wait_recv()

                @pl.when(fed)
                def _():
                    send_ring(k, ll, sgn).wait_recv()
                    add_into(k, 0, ll, (hop2p, hop2m, land))

                @pl.when(jnp.logical_not(fed))
                def _():
                    add_into(k, 0, ll, (hop2p, hop2m))

                send_ring(k, ll, sgn).start()

    def send_wide(k, ll, sgn):
        land, sem = (widep, widep_recv) if sgn == 1 else (widem, widem_recv)
        return remote(
            wide.at[k, ll], land.at[k, ll], wide_send.at[k, ll], sem.at[k, ll], zdev[sgn]
        )

    def ring_wide(t, sgn):
        valid, ll = target_place(t, sgn)
        fed = jnp.logical_or(t < 7, jnp.logical_and(t == 7, side(ll) == sgn))
        land = widep if sgn == 1 else widem

        @pl.when(valid)
        def _():
            for k in (1, 0):
                @pl.when(fed)
                def _():
                    send_wide(k, ll, sgn).wait_recv()
                    wide[k, ll] = (wide[k, ll].astype(F32) + land[k, ll].astype(F32)).astype(BF16)

                send_wide(k, ll, sgn).start()

    def end_ref(k, dy):
        return wide.at[k, low, (y + 4 + dy) % 4]

    def send_end1(k):
        sgn = 2 * k - 1
        return remote(end_ref(k, 2), end1.at[k], end_send.at[0, k], end1_recv.at[k], ydev[sgn])

    def send_end2(k, sgn):
        land, sem = (end2p, end2p_recv) if sgn == 1 else (end2m, end2m_recv)
        return remote(
            end_ref(k, sgn), land.at[k], end_send.at[(3 - sgn) // 2, k], sem.at[k], ydev[sgn]
        )

    def end_wide():
        for k in (1, 0):
            send_wide(k, low, 1).wait_recv()
            send_wide(k, low, -1).wait_recv()
            value = wide[k, low].astype(F32)
            for ref in (widep, widem):
                value = value + ref[k, low].astype(F32)
            wide[k, low] = value.astype(BF16)
            send_end1(k).start()
            send_end2(k, 1 - 2 * k).start()
        for k in (1, 0):
            sgn = 2 * k - 1
            send_end1(k).wait_recv()
            place = (y + 4 + sgn) % 4
            value = wide[k, low, place].astype(F32) + end1[k].astype(F32)
            wide[k, low, place] = value.astype(BF16)
            send_end2(k, sgn).start()

    for k in (1, 0):
        weight_grad(k)
        begin_sum(k)

    def sum_step(i, carry):
        later = 8 - AHEAD - i

        @pl.when(later >= 1)
        def _():
            for k in (1, 0):
                for sgn in (1, -1):
                    begin_y(k, later, sgn)

        @pl.when(later == 0)
        def _():
            for k in (1, 0):
                begin_y(k, 0, 1)

        @pl.when(i < 8)
        def _():
            for sgn in (1, -1):
                ring_wide(8 - i, sgn)
            for sgn in (1, -1):
                middle_y(8 - i, sgn)

        @pl.when(i == 8)
        def _():
            middle_y(0, 1)

        @pl.when(jnp.logical_and(i >= 1, i < 9))
        def _():
            for sgn in (1, -1):
                ring_sum(9 - i, sgn)

        return carry

    lax.fori_loop(0, 9, sum_step, 0)
    pl.when(home)(end_wide)

    pass_tally(10, ydev[1]).wait_recv()
    scale = 127.0 / sum(tally[i] for i in range(8, 12))[0:1, 0:1]

    def send_final():
        return remote(final.at[0], final.at[1], final_send.at[0], final_recv.at[0], sister)

    @pl.when(home)
    def _():
        def total(k, put):
            for sgn in (1, -1):
                send_hop2(k, low, sgn).wait_recv()
                send_ring(k, low, sgn).wait_recv()
            value = partial[k, here].astype(F32)
            for ref in (hop2p, hop2m, ringp, ringm):
                value = value + ref[k, low].astype(F32)
            send_end2(k, 1).wait_recv()
            send_end2(k, -1).wait_recv()
            rest = wide[k, low, y].astype(F32)
            for ref in (end2p, end2m):
                rest = rest + ref[k].astype(F32)
            put[0, :, :SPLIT] = value * scale
            put[0, :, SPLIT:] = rest * scale

        total(1 - core, final)
        send_final().start()
        total(core, out)
        send_final().wait_send()

    @pl.when(jnp.logical_not(home))
    def _():
        send_final().wait_recv()
        out[0] = final[1]

    @pl.when(jnp.logical_not(home))
    def _():
        lend_weight().wait_send()
        lend_inputs().wait_send()

    cross_inputs(0, TOK).wait_send()

    @pl.when(jnp.logical_not(last))
    def _():
        for j in range(CHUNKS):
            chain(j, sister).wait_send()

    for i in (0, 1, 2, 3, 4, 5, 6, 8, 9, 10):
        pass_tally(i, sister).wait_send()

    @pl.when(home)
    def _():
        for k in (1, 0):
            send_end1(k).wait_send()
            send_end2(k, 1).wait_send()
            send_end2(k, -1).wait_send()

    def settle(ll, carry):
        zz = core * 8 + ll
        ahead = (z + 16 - zz) % 16
        plus = jnp.logical_or(ahead < 7, jnp.logical_and(ahead == 7, side(ll) == 1))
        back = (16 - ahead) % 16
        minus = jnp.logical_or(back < 7, jnp.logical_and(back == 7, side(ll) == -1))
        for k in (1, 0):
            @pl.when(plus)
            def _():
                gather_z(k, ll, 1).wait_send()

            @pl.when(minus)
            def _():
                gather_z(k, ll, -1).wait_send()

            gather_y(k, y, ll, 1, 0).wait_send()
            gather_y(k, y, ll, -1, 1).wait_send()
            gather_y(k, y, ll, 1, 2).wait_send()
            send_hop1(k, ll, 1).wait_send()
            send_hop2(k, ll, 1).wait_send()
            send_hop2(k, ll, -1).wait_send()

            @pl.when(ahead != 0)
            def _():
                send_ring(k, ll, 1).wait_send()
                send_wide(k, ll, 1).wait_send()

        return carry

    lax.fori_loop(0, 8, settle, 0)


def shards(section_inputs, loss_grads, weight_codes, proj_weight):
    codes = jnp.broadcast_to(weight_codes.astype(F32)[:, :, None], (2, TOK, 128))
    anywhere = pl.BlockSpec(memory_space=pl.ANY)
    vmem = pl.BlockSpec(memory_space=pltpu.VMEM)
    dma = pltpu.SemaphoreType.DMA
    blocks = (2, 8, ROWS, SPLIT)
    slabs = (2, 8, 4, ROWS, REST)
    ends = (2, ROWS, REST)
    return pl.pallas_call(
        kernel,
        out_shape=jax.ShapeDtypeStruct((1, ROWS, HIDDEN), F32),
        in_specs=[anywhere, anywhere, vmem, vmem],
        out_specs=vmem,
        scratch_shapes=[
            pltpu.VMEM((2, 32, ROWS, HIDDEN), BF16),
            pltpu.VMEM((2, TOK, WIDTH), BF16),
            pltpu.VMEM((2, TOK, WIDTH), BF16),
            pltpu.VMEM((2, CHUNKS, TOK, COLS), BF16),
            pltpu.VMEM((CHUNKS, TOK, COLS), BF16),
            pltpu.VMEM((2, 2 * TOK, HIDDEN), BF16),
            pltpu.VMEM((2, TOK, HIDDEN), F32),
            pltpu.VMEM((2, TOK, HIDDEN), F32),
            pltpu.VMEM((2, TOK, 128), F32),
            pltpu.VMEM((2, 32, ROWS, SPLIT), BF16),
            pltpu.VMEM(slabs, BF16),
            pltpu.VMEM(blocks, BF16),
            pltpu.VMEM(blocks, BF16),
            pltpu.VMEM(blocks, BF16),
            pltpu.VMEM(blocks, BF16),
            pltpu.VMEM(blocks, BF16),
            pltpu.VMEM(slabs, BF16),
            pltpu.VMEM(slabs, BF16),
            pltpu.VMEM(ends, BF16),
            pltpu.VMEM(ends, BF16),
            pltpu.VMEM(ends, BF16),
            pltpu.VMEM((2, ROWS, HIDDEN), F32),
            pltpu.VMEM((12, 8, 128), F32),
            pltpu.VMEM((TOK, WIDTH), BF16),
            dma((3,)),
            dma((2, 32)),
            dma((2, 2, 8)),
            dma((3, 2, 8)),
            dma((3,)),
            dma((2,)),
            dma((CHUNKS,)),
            dma((CHUNKS,)),
            dma((2, 8)),
            dma((2, 8)),
            dma((2, 8)),
            dma((2, 8)),
            dma((2, 8)),
            dma((2, 8)),
            dma((2, 8)),
            dma((2,)),
            dma((2,)),
            dma((2,)),
            dma((2, 8)),
            dma((3, 2)),
            dma((3, 2, 8)),
            dma((2, 8)),
            dma((1,)),
            dma((1,)),
            dma((12,)),
            dma((12,)),
        ],
        compiler_params=pltpu.CompilerParams(
            collective_id=0, has_side_effects=True, vmem_limit_bytes=56 * 2**20
        ),
    )(section_inputs[0][None], loss_grads, codes, proj_weight)


def solution(mesh):
    return jax.shard_map(
        shards,
        mesh=mesh,
        in_specs=(
            P("section", None, "dp", None),
            P(None, "dp", None),
            P(None, "dp"),
            P("section", "dp", None),
        ),
        out_specs=P("section", "dp", None),
        check_vma=False,
    )
```

```python
import jax
import jax.numpy as jnp
from jax import lax
from jax.experimental import pallas as pl
from jax.experimental.pallas import tpu as pltpu
from jax.sharding import PartitionSpec as P

MESH = pl.DeviceIdType.MESH
F32 = jnp.float32
BF16 = jnp.bfloat16
EPSILON = 1e-06
TOK = 64
WAVES = 2
PART = TOK // WAVES
WIDTH = 4096
HIDDEN = 512
ROWS = 128
CHUNKS = 8
COLS = WIDTH // CHUNKS
GROUPS = COLS // ROWS
SPLIT = 384
REST = HIDDEN - SPLIT
AHEAD = 1


def device(x, z, core, y):
    return (x * 4 + (z // 8) * 2 + core, y * 8 + z % 8)


def kernel(
    inputs, loss, codes, shard, out,
    weights, units, normed, grads, outgoing, factors, project, slope, inv_rms, flipped, partial, wide,
    hop1, hop2p, hop2m, ringp, ringm, widep, widem, end1, end2p, end2m, final, tally, staged,
    local_sem, gather_recv, gather_z_send, gather_y_send, cross_send, cross_recv,
    chain_send, chain_recv, hop1_recv, hop2p_recv, hop2m_recv, ringp_recv, ringm_recv,
    widep_recv, widem_recv, end1_recv, end2p_recv, end2m_recv, wide_send, end_send,
    sum_y_send, sum_z_send, final_send, final_recv, tally_send, tally_recv,
):
    section = lax.axis_index("section")
    group = lax.axis_index("dp")
    x, half, core = section // 4, (section // 2) % 2, section % 2
    y, low = group // 8, group % 8
    z = half * 8 + low
    sister = device(x, z, 1 - core, y)
    zdev = {s: device(x, (z + 16 + s) % 16, core, y) for s in (1, -1)}
    ydev = {s: device(x, z, core, (y + 4 + s) % 4) for s in (1, -1)}
    home = core == half
    first = jnp.logical_and(x == 3, core == 1)
    last = jnp.logical_and(x == 0, core == 0)
    far = (z + 8) % 16
    next_x = device((x + 3) % 4, z, 1, y)
    prev_x = device((x + 1) % 4, z, 0, y)

    barrier = pltpu.get_barrier_semaphore()

    def greet(target):
        pl.semaphore_signal(barrier, inc=1, device_id=target, device_id_type=MESH)

    for s in (1, -1):
        greet(zdev[s])
        greet(ydev[s])
    greet(sister)

    @pl.when(jnp.logical_not(home))
    def _():
        greet(device(x, far, 0, y))
        greet(device(x, far, 1, y))

    @pl.when(jnp.logical_and(core == 1, x < 3))
    def _():
        greet(prev_x)

    here = y * 8 + low

    def own_weight():
        return pltpu.make_async_copy(shard.at[0], weights.at[core, here], local_sem.at[0])

    def own_inputs():
        return pltpu.make_async_copy(inputs.at[0, half], units.at[core], local_sem.at[1])

    def seed_copy():
        return pltpu.make_async_copy(loss.at[half], staged, local_sem.at[2])

    @pl.when(home)
    def _():
        own_weight().start()
        own_inputs().start()

    seed_copy().start()
    values = codes[...].astype(F32)
    tally[0] = jnp.broadcast_to(
        jnp.sum(jnp.sum(values, axis=1, keepdims=True), axis=0, keepdims=True), (8, 128)
    )
    seed_copy().wait()

    @pl.when(first)
    def _():
        row = jnp.where(half == 0, values[0:1], values[1:2])
        grid = (TOK, TOK)
        diagonal = lax.broadcasted_iota(jnp.int32, grid, 0) == lax.broadcasted_iota(
            jnp.int32, grid, 1
        )
        spread_row = jnp.broadcast_to(row, grid)
        scale = jnp.sum(jnp.where(diagonal, spread_row, 0.0), axis=1, keepdims=True) / 127.0
        for j in range(CHUNKS):
            part = staged[:, j * COLS:(j + 1) * COLS].astype(F32)
            grads[1, j] = (part * scale).astype(BF16)

    pl.semaphore_wait(barrier, 6 + (1 - core) * ((x + 3) // 4))

    def remote(src, dst, send, recv, target):
        return pltpu.make_async_remote_copy(
            src_ref=src, dst_ref=dst, send_sem=send, recv_sem=recv,
            device_id=target, device_id_type=MESH,
        )

    def lend_weight():
        return remote(
            shard.at[0], weights.at[core, here], cross_send.at[0],
            gather_recv.at[core, here], sister,
        )

    def lend_inputs():
        return remote(
            inputs.at[0, half], units.at[core], cross_send.at[1], cross_recv.at[core], sister
        )

    def cross_inputs(first_row, rows):
        part = pl.ds(first_row, rows)
        return remote(
            inputs.at[0, 1 - half, part], units.at[core, part], cross_send.at[2],
            cross_recv.at[core], device(x, far, half, y),
        )

    @pl.when(jnp.logical_not(home))
    def _():
        lend_weight().start()
        lend_inputs().start()

    def block_ref(k, yy, ll):
        return weights.at[k, yy * 8 + ll]

    def gather_z(k, ll, sgn):
        return remote(
            block_ref(k, y, ll), block_ref(k, y, ll), gather_z_send.at[(1 - sgn) // 2, k, ll],
            gather_recv.at[k, y * 8 + ll], zdev[sgn],
        )

    def gather_y(k, yy, ll, sgn, slot):
        return remote(
            block_ref(k, yy, ll), block_ref(k, yy, ll), gather_y_send.at[slot, k, ll],
            gather_recv.at[k, yy * 8 + ll], ydev[sgn],
        )

    def arrived(k, yy, ll):
        remote(
            block_ref(k, yy, ll), block_ref(k, yy, ll), cross_send.at[0],
            gather_recv.at[k, yy * 8 + ll], sister,
        ).wait_recv()

    def side(ll):
        return 1 - 2 * (ll % 2)

    def ring_place(t, sgn):
        zz = (z + 16 - sgn * t) % 16
        return zz // 8 == core, zz % 8

    def spread_y(k, ll):
        gather_y(k, y, ll, 1, 0).start()
        gather_y(k, y, ll, -1, 1).start()

    @pl.when(home)
    def _():
        own_weight().wait()

        def begin(k):
            for sgn in (1, -1):
                gather_z(k, low, sgn).start()
            spread_y(k, low)

        begin(core)
        arrived(1 - core, y, low)
        begin(1 - core)

    def relay_y(t, sgn):
        valid, ll = ring_place(t, sgn)
        valid = jnp.logical_and(valid, jnp.logical_or(t < 8, side(ll) == sgn))

        @pl.when(valid)
        def _():
            for k in (1, 0):
                arrived(k, (y + 3) % 4, ll)

                @pl.when(side(ll) == 1)
                def _():
                    gather_y(k, (y + 3) % 4, ll, 1, 2).start()

                arrived(k, (y + 1) % 4, ll)

                @pl.when(side(ll) == -1)
                def _():
                    gather_y(k, (y + 1) % 4, ll, -1, 2).start()

    def relay_z(t, sgn):
        valid, ll = ring_place(t, sgn)
        valid = jnp.logical_and(valid, jnp.logical_or(t < 8, side(ll) == sgn))
        onward = jnp.logical_or(t < 7, jnp.logical_and(t == 7, side(ll) == sgn))

        @pl.when(valid)
        def _():
            for k in (1, 0):
                arrived(k, y, ll)

                @pl.when(onward)
                def _():
                    gather_z(k, ll, sgn).start()

                spread_y(k, ll)

    def pass_tally(slot, target):
        return remote(
            tally.at[slot], tally.at[slot + 1], tally_send.at[slot], tally_recv.at[slot + 1],
            target,
        )

    pass_tally(0, zdev[1]).start()

    def tally_y(slot):
        pass_tally(slot - 1, ydev[1]).wait_recv()
        pass_tally(slot, ydev[1]).start()

    def gather_step(t, carry):
        @pl.when(jnp.logical_and(core == 1, t % 2 == 1))
        def _():
            cross_inputs(((t - 1) // 2) * (TOK // 4), TOK // 4).start()

        for sgn in (1, -1):
            relay_z(t, sgn)

        @pl.when(t == 1)
        def _():
            relay_y(0, 1)

        @pl.when(t > 1)
        def _():
            for sgn in (1, -1):
                relay_y(t - 1, sgn)

        @pl.when(t < 7)
        def _():
            pass_tally(t - 1, zdev[1]).wait_recv()
            pass_tally(t, zdev[1]).start()

        return carry

    lax.fori_loop(1, 9, gather_step, 0)

    @pl.when(core == 0)
    def _():
        cross_inputs(0, TOK).start()

    for sgn in (1, -1):
        relay_y(8, sgn)

    pass_tally(6, zdev[1]).wait_recv()
    tally[8] = sum(tally[i] for i in range(1, 8)) + tally[0]
    pass_tally(8, ydev[1]).start()

    def ready(k):
        local = jnp.logical_and(home, core == k)

        @pl.when(local)
        def _():
            own_inputs().wait()

        @pl.when(jnp.logical_not(local))
        def _():
            remote(
                units.at[k], units.at[k], cross_send.at[1], cross_recv.at[k], sister
            ).wait_recv()

    def far_arrived(ll, carry):
        for k in (1, 0):
            arrived(k, (y + 2) % 4, ll)
        return carry

    lax.fori_loop(0, 8, far_arrived, 0)

    def weight_chunk(k, j):
        return weights[k, j * GROUPS:(j + 1) * GROUPS].reshape(COLS, HIDDEN)

    def columns(ref, k, j):
        return ref[k, :, j * COLS:(j + 1) * COLS]

    def unrolled(body, carry):
        for j in range(CHUNKS):
            carry = body(j, carry)
        return carry

    def flip(k):
        for j in range(CHUNKS):
            flipped[k, j] = weight_chunk(k, j).T

    def prepare(k):
        ready(k)

        def square(j, acc):
            v = columns(units, k, j).astype(F32)
            return acc + jnp.sum(v * v, axis=-1, keepdims=True)

        total = unrolled(square, jnp.zeros((TOK, 1), F32))
        inv = lax.rsqrt(total / WIDTH + EPSILON)
        inv_rms[k] = jnp.broadcast_to(inv, (TOK, 128))

        def multiply(j, acc):
            row = (columns(units, k, j).astype(F32) * inv).astype(BF16)
            normed[k, :, j * COLS:(j + 1) * COLS] = row
            return acc + jnp.dot(row, weight_chunk(k, j), preferred_element_type=F32)

        value = unrolled(multiply, jnp.zeros((TOK, HIDDEN), F32))
        prob = jax.nn.sigmoid(value)
        project[k] = value
        slope[k] = prob * (1.0 + value * (1.0 - prob))
        factors[k, TOK:] = (value * prob).astype(BF16)

    prepare(1)

    @pl.when(jnp.logical_not(first))
    def _():
        prepare(0)
        flip(1)
        flip(0)

    def rows_of(w):
        return slice(w * PART, (w + 1) * PART)

    def chain(w, j, target):
        part = pl.ds(w * PART, PART)
        return remote(
            outgoing.at[j, part], grads.at[1, j, part], chain_send.at[w, j],
            chain_recv.at[w, j], target,
        )

    def stage(k, w):
        part = rows_of(w)

        def act_grad(j, acc):
            if k == 1:
                @pl.when(jnp.logical_not(first))
                def _():
                    chain(w, j, sister).wait_recv()
            return acc + jnp.dot(
                grads[k, j, part], weight_chunk(k, j), preferred_element_type=F32
            )

        grad_act = unrolled(act_grad, jnp.zeros((PART, HIDDEN), F32))
        grad_proj = (grad_act * slope[k, part]).astype(BF16)
        factors[k, part] = grad_proj
        mean = jnp.sum(grad_proj.astype(F32) * project[k, part], axis=-1, keepdims=True) / WIDTH
        inv = inv_rms[k, part, 0:1]

        def straight(j):
            return lax.dot_general(
                grad_proj, weight_chunk(k, j), (((1,), (1,)), ((), ())),
                preferred_element_type=F32,
            )

        def turned(j):
            return jnp.dot(grad_proj, flipped[k, j], preferred_element_type=F32)

        def in_grad(j, product):
            norm = product(j)
            unit = units[k, part, j * COLS:(j + 1) * COLS].astype(F32) * inv
            result = (grads[k, j, part].astype(F32) + inv * (norm - unit * mean)).astype(BF16)
            if k == 1:
                grads[0, j, part] = result
            else:
                outgoing[j, part] = result

                @pl.when(core == 1)
                def _():
                    chain(w, j, sister).start()

                @pl.when(core == 0)
                def _():
                    chain(w, j, next_x).start()

            return product

        @pl.when(first)
        def _():
            unrolled(in_grad, straight)

        @pl.when(jnp.logical_and(jnp.logical_not(first), jnp.logical_or(k == 1, jnp.logical_not(last))))
        def _():
            unrolled(in_grad, turned)

    stage(1, 0)

    @pl.when(first)
    def _():
        prepare(0)

    stage(0, 0)
    tally_y(9)
    stage(1, 1)
    stage(0, 1)
    tally_y(10)

    def weight_grad(k):
        def rows(j, carry):
            left = jnp.concatenate([columns(normed, k, j), grads[k, j]], axis=0)
            term = lax.dot_general(
                left, factors[k], (((0,), (0,)), ((), ())), preferred_element_type=F32
            )
            term = term.astype(BF16)
            for i in range(GROUPS):
                place = j * GROUPS + i
                block = term[i * ROWS:(i + 1) * ROWS]
                partial[k, place] = block[:, :SPLIT]
                wide[k, place % 8, place // 8] = block[:, SPLIT:]
            return carry

        unrolled(rows, 0)

    def part_ref(k, dy, ll):
        return partial.at[k, ((y + 4 + dy) % 4) * 8 + ll]

    def send_hop1(k, ll, sgn):
        return remote(
            part_ref(k, 2, ll), hop1.at[k, ll], sum_y_send.at[0, k, ll], hop1_recv.at[k, ll],
            ydev[sgn],
        )

    def send_hop2(k, ll, sgn):
        land, sem = (hop2p, hop2p_recv) if sgn == 1 else (hop2m, hop2m_recv)
        return remote(
            part_ref(k, sgn, ll), land.at[k, ll], sum_y_send.at[(3 - sgn) // 2, k, ll],
            sem.at[k, ll], ydev[sgn],
        )

    def send_ring(k, ll, sgn):
        land, sem = (ringp, ringp_recv) if sgn == 1 else (ringm, ringm_recv)
        return remote(
            part_ref(k, 0, ll), land.at[k, ll], sum_z_send.at[k, ll], sem.at[k, ll], zdev[sgn]
        )

    def target_place(t, sgn):
        zz = (z + 16 + sgn * t) % 16
        ll = zz % 8
        valid = jnp.logical_and(zz // 8 == core, jnp.logical_or(t < 8, side(ll) == sgn))
        return valid, ll

    def begin_y(k, t, sgn):
        valid, ll = target_place(t, sgn)

        @pl.when(valid)
        def _():
            @pl.when(side(ll) == 1)
            def _():
                send_hop1(k, ll, 1).start()
                send_hop2(k, ll, -1).start()

            @pl.when(side(ll) == -1)
            def _():
                send_hop1(k, ll, -1).start()
                send_hop2(k, ll, 1).start()

    def begin_sum(k):
        def body(i, carry):
            for sgn in (1, -1):
                begin_y(k, 8 - i, sgn)
            return carry

        lax.fori_loop(0, AHEAD, body, 0)

    def add_into(k, dy, ll, extra):
        index = ((y + 4 + dy) % 4) * 8 + ll
        value = partial[k, index].astype(F32)
        for ref in extra:
            value = value + ref[k, ll].astype(F32)
        partial[k, index] = value.astype(BF16)

    def middle_y(t, sgn):
        valid, ll = target_place(t, sgn)

        @pl.when(valid)
        def _():
            for k in (1, 0):
                send_hop1(k, ll, 1).wait_recv()

                @pl.when(side(ll) == 1)
                def _():
                    add_into(k, 1, ll, (hop1,))
                    send_hop2(k, ll, 1).start()

                @pl.when(side(ll) == -1)
                def _():
                    add_into(k, -1, ll, (hop1,))
                    send_hop2(k, ll, -1).start()

    def ring_sum(t, sgn):
        valid, ll = target_place(t, sgn)
        fed = jnp.logical_or(t < 7, jnp.logical_and(t == 7, side(ll) == sgn))
        land = ringp if sgn == 1 else ringm

        @pl.when(valid)
        def _():
            for k in (1, 0):
                send_hop2(k, ll, 1).wait_recv()
                send_hop2(k, ll, -1).wait_recv()

                @pl.when(fed)
                def _():
                    send_ring(k, ll, sgn).wait_recv()
                    add_into(k, 0, ll, (hop2p, hop2m, land))

                @pl.when(jnp.logical_not(fed))
                def _():
                    add_into(k, 0, ll, (hop2p, hop2m))

                send_ring(k, ll, sgn).start()

    def send_wide(k, ll, sgn):
        land, sem = (widep, widep_recv) if sgn == 1 else (widem, widem_recv)
        return remote(
            wide.at[k, ll], land.at[k, ll], wide_send.at[k, ll], sem.at[k, ll], zdev[sgn]
        )

    def ring_wide(t, sgn):
        valid, ll = target_place(t, sgn)
        fed = jnp.logical_or(t < 7, jnp.logical_and(t == 7, side(ll) == sgn))
        land = widep if sgn == 1 else widem

        @pl.when(valid)
        def _():
            for k in (1, 0):
                @pl.when(fed)
                def _():
                    send_wide(k, ll, sgn).wait_recv()
                    wide[k, ll] = (wide[k, ll].astype(F32) + land[k, ll].astype(F32)).astype(BF16)

                send_wide(k, ll, sgn).start()

    def end_ref(k, dy):
        return wide.at[k, low, (y + 4 + dy) % 4]

    def send_end1(k):
        sgn = 2 * k - 1
        return remote(end_ref(k, 2), end1.at[k], end_send.at[0, k], end1_recv.at[k], ydev[sgn])

    def send_end2(k, sgn):
        land, sem = (end2p, end2p_recv) if sgn == 1 else (end2m, end2m_recv)
        return remote(
            end_ref(k, sgn), land.at[k], end_send.at[(3 - sgn) // 2, k], sem.at[k], ydev[sgn]
        )

    def end_wide():
        for k in (1, 0):
            send_wide(k, low, 1).wait_recv()
            send_wide(k, low, -1).wait_recv()
            value = wide[k, low].astype(F32)
            for ref in (widep, widem):
                value = value + ref[k, low].astype(F32)
            wide[k, low] = value.astype(BF16)
            send_end1(k).start()
            send_end2(k, 1 - 2 * k).start()
        for k in (1, 0):
            sgn = 2 * k - 1
            send_end1(k).wait_recv()
            place = (y + 4 + sgn) % 4
            value = wide[k, low, place].astype(F32) + end1[k].astype(F32)
            wide[k, low, place] = value.astype(BF16)
            send_end2(k, sgn).start()

    for k in (1, 0):
        weight_grad(k)
        begin_sum(k)

    def sum_step(i, carry):
        later = 8 - AHEAD - i

        @pl.when(later >= 1)
        def _():
            for k in (1, 0):
                for sgn in (1, -1):
                    begin_y(k, later, sgn)

        @pl.when(later == 0)
        def _():
            for k in (1, 0):
                begin_y(k, 0, 1)

        @pl.when(i < 8)
        def _():
            for sgn in (1, -1):
                ring_wide(8 - i, sgn)
            for sgn in (1, -1):
                middle_y(8 - i, sgn)

        @pl.when(i == 8)
        def _():
            middle_y(0, 1)

        @pl.when(jnp.logical_and(i >= 1, i < 9))
        def _():
            for sgn in (1, -1):
                ring_sum(9 - i, sgn)

        return carry

    lax.fori_loop(0, 9, sum_step, 0)
    pl.when(home)(end_wide)

    pass_tally(10, ydev[1]).wait_recv()
    scale = 127.0 / sum(tally[i] for i in range(8, 12))[0:1, 0:1]

    def send_final():
        return remote(final.at[0], final.at[1], final_send.at[0], final_recv.at[0], sister)

    @pl.when(home)
    def _():
        def total(k, put):
            for sgn in (1, -1):
                send_hop2(k, low, sgn).wait_recv()
                send_ring(k, low, sgn).wait_recv()
            value = partial[k, here].astype(F32)
            for ref in (hop2p, hop2m, ringp, ringm):
                value = value + ref[k, low].astype(F32)
            send_end2(k, 1).wait_recv()
            send_end2(k, -1).wait_recv()
            rest = wide[k, low, y].astype(F32)
            for ref in (end2p, end2m):
                rest = rest + ref[k].astype(F32)
            put[0, :, :SPLIT] = value * scale
            put[0, :, SPLIT:] = rest * scale

        total(1 - core, final)
        send_final().start()
        total(core, out)
        send_final().wait_send()

    @pl.when(jnp.logical_not(home))
    def _():
        send_final().wait_recv()
        out[0] = final[1]

    @pl.when(jnp.logical_not(home))
    def _():
        lend_weight().wait_send()
        lend_inputs().wait_send()

    cross_inputs(0, TOK).wait_send()

    @pl.when(jnp.logical_not(last))
    def _():
        for w in range(WAVES):
            for j in range(CHUNKS):
                chain(w, j, sister).wait_send()

    for i in (0, 1, 2, 3, 4, 5, 6, 8, 9, 10):
        pass_tally(i, sister).wait_send()

    @pl.when(home)
    def _():
        for k in (1, 0):
            send_end1(k).wait_send()
            send_end2(k, 1).wait_send()
            send_end2(k, -1).wait_send()

    def settle(ll, carry):
        zz = core * 8 + ll
        ahead = (z + 16 - zz) % 16
        plus = jnp.logical_or(ahead < 7, jnp.logical_and(ahead == 7, side(ll) == 1))
        back = (16 - ahead) % 16
        minus = jnp.logical_or(back < 7, jnp.logical_and(back == 7, side(ll) == -1))
        for k in (1, 0):
            @pl.when(plus)
            def _():
                gather_z(k, ll, 1).wait_send()

            @pl.when(minus)
            def _():
                gather_z(k, ll, -1).wait_send()

            gather_y(k, y, ll, 1, 0).wait_send()
            gather_y(k, y, ll, -1, 1).wait_send()
            gather_y(k, y, ll, 1, 2).wait_send()
            send_hop1(k, ll, 1).wait_send()
            send_hop2(k, ll, 1).wait_send()
            send_hop2(k, ll, -1).wait_send()

            @pl.when(ahead != 0)
            def _():
                send_ring(k, ll, 1).wait_send()
                send_wide(k, ll, 1).wait_send()

        return carry

    lax.fori_loop(0, 8, settle, 0)


def shards(section_inputs, loss_grads, weight_codes, proj_weight):
    anywhere = pl.BlockSpec(memory_space=pl.ANY)
    vmem = pl.BlockSpec(memory_space=pltpu.VMEM)
    dma = pltpu.SemaphoreType.DMA
    blocks = (2, 8, ROWS, SPLIT)
    slabs = (2, 8, 4, ROWS, REST)
    ends = (2, ROWS, REST)
    return pl.pallas_call(
        kernel,
        out_shape=jax.ShapeDtypeStruct((1, ROWS, HIDDEN), F32),
        in_specs=[anywhere, anywhere, vmem, vmem],
        out_specs=vmem,
        scratch_shapes=[
            pltpu.VMEM((2, 32, ROWS, HIDDEN), BF16),
            pltpu.VMEM((2, TOK, WIDTH), BF16),
            pltpu.VMEM((2, TOK, WIDTH), BF16),
            pltpu.VMEM((2, CHUNKS, TOK, COLS), BF16),
            pltpu.VMEM((CHUNKS, TOK, COLS), BF16),
            pltpu.VMEM((2, 2 * TOK, HIDDEN), BF16),
            pltpu.VMEM((2, TOK, HIDDEN), F32),
            pltpu.VMEM((2, TOK, HIDDEN), F32),
            pltpu.VMEM((2, TOK, 128), F32),
            pltpu.VMEM((2, CHUNKS, HIDDEN, COLS), BF16),
            pltpu.VMEM((2, 32, ROWS, SPLIT), BF16),
            pltpu.VMEM(slabs, BF16),
            pltpu.VMEM(blocks, BF16),
            pltpu.VMEM(blocks, BF16),
            pltpu.VMEM(blocks, BF16),
            pltpu.VMEM(blocks, BF16),
            pltpu.VMEM(blocks, BF16),
            pltpu.VMEM(slabs, BF16),
            pltpu.VMEM(slabs, BF16),
            pltpu.VMEM(ends, BF16),
            pltpu.VMEM(ends, BF16),
            pltpu.VMEM(ends, BF16),
            pltpu.VMEM((2, ROWS, HIDDEN), F32),
            pltpu.VMEM((12, 8, 128), F32),
            pltpu.VMEM((TOK, WIDTH), BF16),
            dma((3,)),
            dma((2, 32)),
            dma((2, 2, 8)),
            dma((3, 2, 8)),
            dma((3,)),
            dma((2,)),
            dma((WAVES, CHUNKS)),
            dma((WAVES, CHUNKS)),
            dma((2, 8)),
            dma((2, 8)),
            dma((2, 8)),
            dma((2, 8)),
            dma((2, 8)),
            dma((2, 8)),
            dma((2, 8)),
            dma((2,)),
            dma((2,)),
            dma((2,)),
            dma((2, 8)),
            dma((3, 2)),
            dma((3, 2, 8)),
            dma((2, 8)),
            dma((1,)),
            dma((1,)),
            dma((12,)),
            dma((12,)),
        ],
        compiler_params=pltpu.CompilerParams(
            collective_id=0, has_side_effects=True, vmem_limit_bytes=56 * 2**20
        ),
    )(section_inputs[0][None], loss_grads, weight_codes, proj_weight)


def solution(mesh):
    return jax.shard_map(
        shards,
        mesh=mesh,
        in_specs=(
            P("section", None, "dp", None),
            P(None, "dp", None),
            P(None, "dp"),
            P("section", "dp", None),
        ),
        out_specs=P("section", "dp", None),
        check_vma=False,
    )
```

```python
import jax
import jax.numpy as jnp
from jax import lax
from jax.experimental import pallas as pl
from jax.experimental.pallas import tpu as pltpu
from jax.sharding import PartitionSpec as P

MESH = pl.DeviceIdType.MESH
F32 = jnp.float32
BF16 = jnp.bfloat16
EPSILON = 1e-06
TOK = 64
WAVES = 2
PART = TOK // WAVES
WIDTH = 4096
HIDDEN = 512
ROWS = 128
CHUNKS = 8
COLS = WIDTH // CHUNKS
GROUPS = COLS // ROWS
SPLIT = 384
REST = HIDDEN - SPLIT
AHEAD = 1


def device(x, z, core, y):
    return (x * 4 + (z // 8) * 2 + core, y * 8 + z % 8)


def kernel(
    inputs, loss, codes, shard, out,
    weights, units, normed, grads, outgoing, factors, project, slope, inv_rms, flipped, partial, wide,
    hop1, hop2p, hop2m, ringp, ringm, widep, widem, end1, end2p, end2m, final, tally, staged,
    local_sem, gather_recv, gather_z_send, gather_y_send, cross_send, cross_recv,
    chain_send, chain_recv, hop1_recv, hop2p_recv, hop2m_recv, ringp_recv, ringm_recv,
    widep_recv, widem_recv, end1_recv, end2p_recv, end2m_recv, wide_send, end_send,
    sum_y_send, sum_z_send, final_send, final_recv, tally_send, tally_recv,
):
    section = lax.axis_index("section")
    group = lax.axis_index("dp")
    x, half, core = section // 4, (section // 2) % 2, section % 2
    y, low = group // 8, group % 8
    z = half * 8 + low
    sister = device(x, z, 1 - core, y)
    zdev = {s: device(x, (z + 16 + s) % 16, core, y) for s in (1, -1)}
    ydev = {s: device(x, z, core, (y + 4 + s) % 4) for s in (1, -1)}
    home = core == half
    first = jnp.logical_and(x == 3, core == 1)
    last = jnp.logical_and(x == 0, core == 0)
    far = (z + 8) % 16
    next_x = device((x + 3) % 4, z, 1, y)
    prev_x = device((x + 1) % 4, z, 0, y)

    barrier = pltpu.get_barrier_semaphore()

    def greet(target):
        pl.semaphore_signal(barrier, inc=1, device_id=target, device_id_type=MESH)

    for s in (1, -1):
        greet(zdev[s])
        greet(ydev[s])
    greet(sister)

    @pl.when(jnp.logical_not(home))
    def _():
        greet(device(x, far, 0, y))
        greet(device(x, far, 1, y))

    @pl.when(jnp.logical_and(core == 1, x < 3))
    def _():
        greet(prev_x)

    here = y * 8 + low

    def own_weight():
        return pltpu.make_async_copy(shard.at[0], weights.at[core, here], local_sem.at[0])

    def own_inputs():
        return pltpu.make_async_copy(inputs.at[0, half], units.at[core], local_sem.at[1])

    def seed_copy():
        return pltpu.make_async_copy(loss.at[half], staged, local_sem.at[2])

    @pl.when(home)
    def _():
        own_weight().start()
        own_inputs().start()

    seed_copy().start()
    values = codes[...].astype(F32)
    tally[0] = jnp.broadcast_to(
        jnp.sum(jnp.sum(values, axis=1, keepdims=True), axis=0, keepdims=True), (8, 128)
    )
    seed_copy().wait()

    @pl.when(first)
    def _():
        row = jnp.where(half == 0, values[0:1], values[1:2])
        grid = (TOK, TOK)
        diagonal = lax.broadcasted_iota(jnp.int32, grid, 0) == lax.broadcasted_iota(
            jnp.int32, grid, 1
        )
        spread_row = jnp.broadcast_to(row, grid)
        scale = jnp.sum(jnp.where(diagonal, spread_row, 0.0), axis=1, keepdims=True) / 127.0
        for j in range(CHUNKS):
            part = staged[:, j * COLS:(j + 1) * COLS].astype(F32)
            grads[1, j] = (part * scale).astype(BF16)

    pl.semaphore_wait(barrier, 6 + (1 - core) * ((x + 3) // 4))

    def remote(src, dst, send, recv, target):
        return pltpu.make_async_remote_copy(
            src_ref=src, dst_ref=dst, send_sem=send, recv_sem=recv,
            device_id=target, device_id_type=MESH,
        )

    def lend_weight():
        return remote(
            shard.at[0], weights.at[core, here], cross_send.at[0],
            gather_recv.at[core, here], sister,
        )

    def lend_inputs():
        return remote(
            inputs.at[0, half], units.at[core], cross_send.at[1], cross_recv.at[core], sister
        )

    def cross_inputs(first_row, rows):
        part = pl.ds(first_row, rows)
        return remote(
            inputs.at[0, 1 - half, :, part], units.at[core, :, part], cross_send.at[2],
            cross_recv.at[core], device(x, far, half, y),
        )

    @pl.when(jnp.logical_not(home))
    def _():
        lend_weight().start()
        lend_inputs().start()

    def block_ref(k, yy, ll):
        return weights.at[k, yy * 8 + ll]

    def gather_z(k, ll, sgn):
        return remote(
            block_ref(k, y, ll), block_ref(k, y, ll), gather_z_send.at[(1 - sgn) // 2, k, ll],
            gather_recv.at[k, y * 8 + ll], zdev[sgn],
        )

    def gather_y(k, yy, ll, sgn, slot):
        return remote(
            block_ref(k, yy, ll), block_ref(k, yy, ll), gather_y_send.at[slot, k, ll],
            gather_recv.at[k, yy * 8 + ll], ydev[sgn],
        )

    def arrived(k, yy, ll):
        remote(
            block_ref(k, yy, ll), block_ref(k, yy, ll), cross_send.at[0],
            gather_recv.at[k, yy * 8 + ll], sister,
        ).wait_recv()

    def side(ll):
        return 1 - 2 * (ll % 2)

    def ring_place(t, sgn):
        zz = (z + 16 - sgn * t) % 16
        return zz // 8 == core, zz % 8

    def spread_y(k, ll):
        gather_y(k, y, ll, 1, 0).start()
        gather_y(k, y, ll, -1, 1).start()

    @pl.when(home)
    def _():
        own_weight().wait()

        def begin(k):
            for sgn in (1, -1):
                gather_z(k, low, sgn).start()
            spread_y(k, low)

        begin(core)
        arrived(1 - core, y, low)
        begin(1 - core)

    def relay_y(t, sgn):
        valid, ll = ring_place(t, sgn)
        valid = jnp.logical_and(valid, jnp.logical_or(t < 8, side(ll) == sgn))

        @pl.when(valid)
        def _():
            for k in (1, 0):
                arrived(k, (y + 3) % 4, ll)

                @pl.when(side(ll) == 1)
                def _():
                    gather_y(k, (y + 3) % 4, ll, 1, 2).start()

                arrived(k, (y + 1) % 4, ll)

                @pl.when(side(ll) == -1)
                def _():
                    gather_y(k, (y + 1) % 4, ll, -1, 2).start()

    def relay_z(t, sgn):
        valid, ll = ring_place(t, sgn)
        valid = jnp.logical_and(valid, jnp.logical_or(t < 8, side(ll) == sgn))
        onward = jnp.logical_or(t < 7, jnp.logical_and(t == 7, side(ll) == sgn))

        @pl.when(valid)
        def _():
            for k in (1, 0):
                arrived(k, y, ll)

                @pl.when(onward)
                def _():
                    gather_z(k, ll, sgn).start()

                spread_y(k, ll)

    def pass_tally(slot, target):
        return remote(
            tally.at[slot], tally.at[slot + 1], tally_send.at[slot], tally_recv.at[slot + 1],
            target,
        )

    pass_tally(0, zdev[1]).start()

    def tally_y(slot):
        pass_tally(slot - 1, ydev[1]).wait_recv()
        pass_tally(slot, ydev[1]).start()

    def gather_step(t, carry):
        @pl.when(core == 1)
        def _():
            cross_inputs((t - 1) * COLS, COLS).start()

        for sgn in (1, -1):
            relay_z(t, sgn)

        @pl.when(t == 1)
        def _():
            relay_y(0, 1)

        @pl.when(t > 1)
        def _():
            for sgn in (1, -1):
                relay_y(t - 1, sgn)

        @pl.when(t < 7)
        def _():
            pass_tally(t - 1, zdev[1]).wait_recv()
            pass_tally(t, zdev[1]).start()

        return carry

    lax.fori_loop(1, 9, gather_step, 0)

    @pl.when(core == 0)
    def _():
        cross_inputs(0, WIDTH).start()

    for sgn in (1, -1):
        relay_y(8, sgn)

    pass_tally(6, zdev[1]).wait_recv()
    tally[8] = sum(tally[i] for i in range(1, 8)) + tally[0]
    pass_tally(8, ydev[1]).start()

    def ready(k):
        local = jnp.logical_and(home, core == k)

        @pl.when(local)
        def _():
            own_inputs().wait()

        @pl.when(jnp.logical_not(local))
        def _():
            remote(
                units.at[k], units.at[k], cross_send.at[1], cross_recv.at[k], sister
            ).wait_recv()

    def far_arrived(ll, carry):
        for k in (1, 0):
            arrived(k, (y + 2) % 4, ll)
        return carry

    lax.fori_loop(0, 8, far_arrived, 0)

    def weight_chunk(k, j):
        return weights[k, j * GROUPS:(j + 1) * GROUPS].reshape(COLS, HIDDEN)

    def columns(ref, k, j):
        return ref[k, :, j * COLS:(j + 1) * COLS]

    def unrolled(body, carry):
        for j in range(CHUNKS):
            carry = body(j, carry)
        return carry

    def flip(k):
        for j in range(CHUNKS):
            flipped[k, j] = weight_chunk(k, j).T

    def prepare(k):
        ready(k)

        def square(j, acc):
            v = columns(units, k, j).astype(F32)
            return acc + jnp.sum(v * v, axis=-1, keepdims=True)

        total = unrolled(square, jnp.zeros((TOK, 1), F32))
        inv = lax.rsqrt(total / WIDTH + EPSILON)
        inv_rms[k] = jnp.broadcast_to(inv, (TOK, 128))

        def multiply(j, acc):
            row = (columns(units, k, j).astype(F32) * inv).astype(BF16)
            normed[k, :, j * COLS:(j + 1) * COLS] = row
            return acc + jnp.dot(row, weight_chunk(k, j), preferred_element_type=F32)

        value = unrolled(multiply, jnp.zeros((TOK, HIDDEN), F32))
        prob = jax.nn.sigmoid(value)
        project[k] = value
        slope[k] = prob * (1.0 + value * (1.0 - prob))
        factors[k, TOK:] = (value * prob).astype(BF16)

    prepare(1)

    @pl.when(jnp.logical_not(first))
    def _():
        flip(1)
        flip(0)
        prepare(0)

    def rows_of(w):
        return slice(w * PART, (w + 1) * PART)

    def chain(w, j, target):
        part = pl.ds(w * PART, PART)
        return remote(
            outgoing.at[j, part], grads.at[1, j, part], chain_send.at[w, j],
            chain_recv.at[w, j], target,
        )

    def stage(k, w):
        part = rows_of(w)

        def act_grad(j, acc):
            if k == 1:
                @pl.when(jnp.logical_not(first))
                def _():
                    chain(w, j, sister).wait_recv()
            return acc + jnp.dot(
                grads[k, j, part], weight_chunk(k, j), preferred_element_type=F32
            )

        grad_act = unrolled(act_grad, jnp.zeros((PART, HIDDEN), F32))
        grad_proj = (grad_act * slope[k, part]).astype(BF16)
        factors[k, part] = grad_proj
        mean = jnp.sum(grad_proj.astype(F32) * project[k, part], axis=-1, keepdims=True) / WIDTH
        inv = inv_rms[k, part, 0:1]

        def straight(j):
            return lax.dot_general(
                grad_proj, weight_chunk(k, j), (((1,), (1,)), ((), ())),
                preferred_element_type=F32,
            )

        def turned(j):
            return jnp.dot(grad_proj, flipped[k, j], preferred_element_type=F32)

        def in_grad(j, product):
            norm = product(j)
            unit = units[k, part, j * COLS:(j + 1) * COLS].astype(F32) * inv
            result = (grads[k, j, part].astype(F32) + inv * (norm - unit * mean)).astype(BF16)
            if k == 1:
                grads[0, j, part] = result
            else:
                outgoing[j, part] = result

                @pl.when(core == 1)
                def _():
                    chain(w, j, sister).start()

                @pl.when(core == 0)
                def _():
                    chain(w, j, next_x).start()

            return product

        @pl.when(first)
        def _():
            unrolled(in_grad, straight)

        @pl.when(jnp.logical_and(jnp.logical_not(first), jnp.logical_or(k == 1, jnp.logical_not(last))))
        def _():
            unrolled(in_grad, turned)

    stage(1, 0)

    @pl.when(first)
    def _():
        prepare(0)

    stage(0, 0)
    tally_y(9)
    stage(1, 1)
    stage(0, 1)
    tally_y(10)

    def weight_grad(k):
        def rows(j, carry):
            left = jnp.concatenate([columns(normed, k, j), grads[k, j]], axis=0)
            term = lax.dot_general(
                left, factors[k], (((0,), (0,)), ((), ())), preferred_element_type=F32
            )
            term = term.astype(BF16)
            for i in range(GROUPS):
                place = j * GROUPS + i
                block = term[i * ROWS:(i + 1) * ROWS]
                partial[k, place] = block[:, :SPLIT]
                wide[k, place % 8, place // 8] = block[:, SPLIT:]
            return carry

        unrolled(rows, 0)

    def part_ref(k, dy, ll):
        return partial.at[k, ((y + 4 + dy) % 4) * 8 + ll]

    def send_hop1(k, ll, sgn):
        return remote(
            part_ref(k, 2, ll), hop1.at[k, ll], sum_y_send.at[0, k, ll], hop1_recv.at[k, ll],
            ydev[sgn],
        )

    def send_hop2(k, ll, sgn):
        land, sem = (hop2p, hop2p_recv) if sgn == 1 else (hop2m, hop2m_recv)
        return remote(
            part_ref(k, sgn, ll), land.at[k, ll], sum_y_send.at[(3 - sgn) // 2, k, ll],
            sem.at[k, ll], ydev[sgn],
        )

    def send_ring(k, ll, sgn):
        land, sem = (ringp, ringp_recv) if sgn == 1 else (ringm, ringm_recv)
        return remote(
            part_ref(k, 0, ll), land.at[k, ll], sum_z_send.at[k, ll], sem.at[k, ll], zdev[sgn]
        )

    def target_place(t, sgn):
        zz = (z + 16 + sgn * t) % 16
        ll = zz % 8
        valid = jnp.logical_and(zz // 8 == core, jnp.logical_or(t < 8, side(ll) == sgn))
        return valid, ll

    def begin_y(k, t, sgn):
        valid, ll = target_place(t, sgn)

        @pl.when(valid)
        def _():
            @pl.when(side(ll) == 1)
            def _():
                send_hop1(k, ll, 1).start()
                send_hop2(k, ll, -1).start()

            @pl.when(side(ll) == -1)
            def _():
                send_hop1(k, ll, -1).start()
                send_hop2(k, ll, 1).start()

    def begin_sum(k):
        def body(i, carry):
            for sgn in (1, -1):
                begin_y(k, 8 - i, sgn)
            return carry

        lax.fori_loop(0, AHEAD, body, 0)

    def add_into(k, dy, ll, extra):
        index = ((y + 4 + dy) % 4) * 8 + ll
        value = partial[k, index].astype(F32)
        for ref in extra:
            value = value + ref[k, ll].astype(F32)
        partial[k, index] = value.astype(BF16)

    def middle_y(t, sgn):
        valid, ll = target_place(t, sgn)

        @pl.when(valid)
        def _():
            for k in (1, 0):
                send_hop1(k, ll, 1).wait_recv()

                @pl.when(side(ll) == 1)
                def _():
                    add_into(k, 1, ll, (hop1,))
                    send_hop2(k, ll, 1).start()

                @pl.when(side(ll) == -1)
                def _():
                    add_into(k, -1, ll, (hop1,))
                    send_hop2(k, ll, -1).start()

    def ring_sum(t, sgn):
        valid, ll = target_place(t, sgn)
        fed = jnp.logical_or(t < 7, jnp.logical_and(t == 7, side(ll) == sgn))
        land = ringp if sgn == 1 else ringm

        @pl.when(valid)
        def _():
            for k in (1, 0):
                send_hop2(k, ll, 1).wait_recv()
                send_hop2(k, ll, -1).wait_recv()

                @pl.when(fed)
                def _():
                    send_ring(k, ll, sgn).wait_recv()
                    add_into(k, 0, ll, (hop2p, hop2m, land))

                @pl.when(jnp.logical_not(fed))
                def _():
                    add_into(k, 0, ll, (hop2p, hop2m))

                send_ring(k, ll, sgn).start()

    def send_wide(k, ll, sgn):
        land, sem = (widep, widep_recv) if sgn == 1 else (widem, widem_recv)
        return remote(
            wide.at[k, ll], land.at[k, ll], wide_send.at[k, ll], sem.at[k, ll], zdev[sgn]
        )

    def ring_wide(t, sgn):
        valid, ll = target_place(t, sgn)
        fed = jnp.logical_or(t < 7, jnp.logical_and(t == 7, side(ll) == sgn))
        land = widep if sgn == 1 else widem

        @pl.when(valid)
        def _():
            for k in (1, 0):
                @pl.when(fed)
                def _():
                    send_wide(k, ll, sgn).wait_recv()
                    wide[k, ll] = (wide[k, ll].astype(F32) + land[k, ll].astype(F32)).astype(BF16)

                send_wide(k, ll, sgn).start()

    def end_ref(k, dy):
        return wide.at[k, low, (y + 4 + dy) % 4]

    def send_end1(k):
        sgn = 2 * k - 1
        return remote(end_ref(k, 2), end1.at[k], end_send.at[0, k], end1_recv.at[k], ydev[sgn])

    def send_end2(k, sgn):
        land, sem = (end2p, end2p_recv) if sgn == 1 else (end2m, end2m_recv)
        return remote(
            end_ref(k, sgn), land.at[k], end_send.at[(3 - sgn) // 2, k], sem.at[k], ydev[sgn]
        )

    def end_wide():
        for k in (1, 0):
            send_wide(k, low, 1).wait_recv()
            send_wide(k, low, -1).wait_recv()
            value = wide[k, low].astype(F32)
            for ref in (widep, widem):
                value = value + ref[k, low].astype(F32)
            wide[k, low] = value.astype(BF16)
            send_end1(k).start()
            send_end2(k, 1 - 2 * k).start()

    def end_wide_later():
        for k in (1, 0):
            sgn = 2 * k - 1
            send_end1(k).wait_recv()
            place = (y + 4 + sgn) % 4
            value = wide[k, low, place].astype(F32) + end1[k].astype(F32)
            wide[k, low, place] = value.astype(BF16)
            send_end2(k, sgn).start()

    for k in (1, 0):
        weight_grad(k)
        begin_sum(k)

    def sum_step(i, carry):
        @pl.when(i < 8)
        def _():
            for sgn in (1, -1):
                ring_wide(8 - i, sgn)
            for sgn in (1, -1):
                middle_y(8 - i, sgn)

        later = 8 - AHEAD - i

        @pl.when(later >= 1)
        def _():
            for k in (1, 0):
                for sgn in (1, -1):
                    begin_y(k, later, sgn)

        @pl.when(later == 0)
        def _():
            for k in (1, 0):
                begin_y(k, 0, 1)

        pl.when(jnp.logical_and(i == 8, home))(end_wide)

        @pl.when(i == 8)
        def _():
            middle_y(0, 1)

        @pl.when(jnp.logical_and(i >= 1, i < 9))
        def _():
            for sgn in (1, -1):
                ring_sum(9 - i, sgn)

        return carry

    lax.fori_loop(0, 9, sum_step, 0)
    pl.when(home)(end_wide_later)

    pass_tally(10, ydev[1]).wait_recv()
    scale = 127.0 / sum(tally[i] for i in range(8, 12))[0:1, 0:1]

    def send_final():
        return remote(final.at[0], final.at[1], final_send.at[0], final_recv.at[0], sister)

    @pl.when(home)
    def _():
        def total(k, put):
            for sgn in (1, -1):
                send_hop2(k, low, sgn).wait_recv()
                send_ring(k, low, sgn).wait_recv()
            value = partial[k, here].astype(F32)
            for ref in (hop2p, hop2m, ringp, ringm):
                value = value + ref[k, low].astype(F32)
            send_end2(k, 1).wait_recv()
            send_end2(k, -1).wait_recv()
            rest = wide[k, low, y].astype(F32)
            for ref in (end2p, end2m):
                rest = rest + ref[k].astype(F32)
            put[0, :, :SPLIT] = value * scale
            put[0, :, SPLIT:] = rest * scale

        total(1 - core, final)
        send_final().start()
        total(core, out)
        send_final().wait_send()

    @pl.when(jnp.logical_not(home))
    def _():
        send_final().wait_recv()
        out[0] = final[1]

    @pl.when(jnp.logical_not(home))
    def _():
        lend_weight().wait_send()
        lend_inputs().wait_send()

    cross_inputs(0, WIDTH).wait_send()

    @pl.when(jnp.logical_not(last))
    def _():
        for w in range(WAVES):
            for j in range(CHUNKS):
                chain(w, j, sister).wait_send()

    for i in (0, 1, 2, 3, 4, 5, 6, 8, 9, 10):
        pass_tally(i, sister).wait_send()

    @pl.when(home)
    def _():
        for k in (1, 0):
            send_end1(k).wait_send()
            send_end2(k, 1).wait_send()
            send_end2(k, -1).wait_send()

    def settle(ll, carry):
        zz = core * 8 + ll
        ahead = (z + 16 - zz) % 16
        plus = jnp.logical_or(ahead < 7, jnp.logical_and(ahead == 7, side(ll) == 1))
        back = (16 - ahead) % 16
        minus = jnp.logical_or(back < 7, jnp.logical_and(back == 7, side(ll) == -1))
        for k in (1, 0):
            @pl.when(plus)
            def _():
                gather_z(k, ll, 1).wait_send()

            @pl.when(minus)
            def _():
                gather_z(k, ll, -1).wait_send()

            gather_y(k, y, ll, 1, 0).wait_send()
            gather_y(k, y, ll, -1, 1).wait_send()
            gather_y(k, y, ll, 1, 2).wait_send()
            send_hop1(k, ll, 1).wait_send()
            send_hop2(k, ll, 1).wait_send()
            send_hop2(k, ll, -1).wait_send()

            @pl.when(ahead != 0)
            def _():
                send_ring(k, ll, 1).wait_send()
                send_wide(k, ll, 1).wait_send()

        return carry

    lax.fori_loop(0, 8, settle, 0)


def shards(section_inputs, loss_grads, weight_codes, proj_weight):
    anywhere = pl.BlockSpec(memory_space=pl.ANY)
    vmem = pl.BlockSpec(memory_space=pltpu.VMEM)
    dma = pltpu.SemaphoreType.DMA
    blocks = (2, 8, ROWS, SPLIT)
    slabs = (2, 8, 4, ROWS, REST)
    ends = (2, ROWS, REST)
    return pl.pallas_call(
        kernel,
        out_shape=jax.ShapeDtypeStruct((1, ROWS, HIDDEN), F32),
        in_specs=[anywhere, anywhere, vmem, vmem],
        out_specs=vmem,
        scratch_shapes=[
            pltpu.VMEM((2, 32, ROWS, HIDDEN), BF16),
            pltpu.VMEM((2, TOK, WIDTH), BF16),
            pltpu.VMEM((2, TOK, WIDTH), BF16),
            pltpu.VMEM((2, CHUNKS, TOK, COLS), BF16),
            pltpu.VMEM((CHUNKS, TOK, COLS), BF16),
            pltpu.VMEM((2, 2 * TOK, HIDDEN), BF16),
            pltpu.VMEM((2, TOK, HIDDEN), F32),
            pltpu.VMEM((2, TOK, HIDDEN), F32),
            pltpu.VMEM((2, TOK, 128), F32),
            pltpu.VMEM((2, CHUNKS, HIDDEN, COLS), BF16),
            pltpu.VMEM((2, 32, ROWS, SPLIT), BF16),
            pltpu.VMEM(slabs, BF16),
            pltpu.VMEM(blocks, BF16),
            pltpu.VMEM(blocks, BF16),
            pltpu.VMEM(blocks, BF16),
            pltpu.VMEM(blocks, BF16),
            pltpu.VMEM(blocks, BF16),
            pltpu.VMEM(slabs, BF16),
            pltpu.VMEM(slabs, BF16),
            pltpu.VMEM(ends, BF16),
            pltpu.VMEM(ends, BF16),
            pltpu.VMEM(ends, BF16),
            pltpu.VMEM((2, ROWS, HIDDEN), F32),
            pltpu.VMEM((12, 8, 128), F32),
            pltpu.VMEM((TOK, WIDTH), BF16),
            dma((3,)),
            dma((2, 32)),
            dma((2, 2, 8)),
            dma((3, 2, 8)),
            dma((3,)),
            dma((2,)),
            dma((WAVES, CHUNKS)),
            dma((WAVES, CHUNKS)),
            dma((2, 8)),
            dma((2, 8)),
            dma((2, 8)),
            dma((2, 8)),
            dma((2, 8)),
            dma((2, 8)),
            dma((2, 8)),
            dma((2,)),
            dma((2,)),
            dma((2,)),
            dma((2, 8)),
            dma((3, 2)),
            dma((3, 2, 8)),
            dma((2, 8)),
            dma((1,)),
            dma((1,)),
            dma((12,)),
            dma((12,)),
        ],
        compiler_params=pltpu.CompilerParams(
            collective_id=0, has_side_effects=True, vmem_limit_bytes=56 * 2**20
        ),
    )(section_inputs[0][None], loss_grads, weight_codes, proj_weight)


def solution(mesh):
    return jax.shard_map(
        shards,
        mesh=mesh,
        in_specs=(
            P("section", None, "dp", None),
            P(None, "dp", None),
            P(None, "dp"),
            P("section", "dp", None),
        ),
        out_specs=P("section", "dp", None),
        check_vma=False,
    )
```

```python
import jax
import jax.numpy as jnp
from jax import lax
from jax.experimental import pallas as pl
from jax.experimental.pallas import tpu as pltpu
from jax.sharding import PartitionSpec as P

MESH = pl.DeviceIdType.MESH
F32 = jnp.float32
BF16 = jnp.bfloat16
EPSILON = 1e-06
TOK = 64
WAVES = 2
PART = TOK // WAVES
WIDTH = 4096
HIDDEN = 512
ROWS = 128
CHUNKS = 8
COLS = WIDTH // CHUNKS
GROUPS = COLS // ROWS
SPLIT = 384
REST = HIDDEN - SPLIT
AHEAD = 1


def device(x, z, core, y):
    return (x * 4 + (z // 8) * 2 + core, y * 8 + z % 8)


def kernel(
    inputs, loss, codes, shard, out,
    weights, units, normed, grads, outgoing, factors, project, slope, inv_rms, flipped, partial, wide,
    hop1, hop2p, hop2m, ringp, ringm, widep, widem, end1, end2p, end2m, final, tally, staged,
    local_sem, gather_recv, gather_z_send, gather_y_send, cross_send, cross_recv,
    chain_send, chain_recv, hop1_recv, hop2p_recv, hop2m_recv, ringp_recv, ringm_recv,
    widep_recv, widem_recv, end1_recv, end2p_recv, end2m_recv, wide_send, end_send,
    sum_y_send, sum_z_send, final_send, final_recv, tally_send, tally_recv,
):
    section = lax.axis_index("section")
    group = lax.axis_index("dp")
    x, half, core = section // 4, (section // 2) % 2, section % 2
    y, low = group // 8, group % 8
    z = half * 8 + low
    sister = device(x, z, 1 - core, y)
    zdev = {s: device(x, (z + 16 + s) % 16, core, y) for s in (1, -1)}
    ydev = {s: device(x, z, core, (y + 4 + s) % 4) for s in (1, -1)}
    home = core == half
    first = jnp.logical_and(x == 3, core == 1)
    last = jnp.logical_and(x == 0, core == 0)
    far = (z + 8) % 16
    next_x = device((x + 3) % 4, z, 1, y)
    prev_x = device((x + 1) % 4, z, 0, y)

    barrier = pltpu.get_barrier_semaphore()

    def greet(target):
        pl.semaphore_signal(barrier, inc=1, device_id=target, device_id_type=MESH)

    for s in (1, -1):
        greet(zdev[s])
        greet(ydev[s])
    greet(sister)

    @pl.when(jnp.logical_not(home))
    def _():
        greet(device(x, far, 0, y))
        greet(device(x, far, 1, y))

    @pl.when(jnp.logical_and(core == 1, x < 3))
    def _():
        greet(prev_x)

    here = y * 8 + low

    def own_weight():
        return pltpu.make_async_copy(shard.at[0], weights.at[core, here], local_sem.at[0])

    def own_inputs():
        return pltpu.make_async_copy(inputs.at[0, half], units.at[core], local_sem.at[1])

    def seed_copy():
        return pltpu.make_async_copy(loss.at[half], staged, local_sem.at[2])

    @pl.when(home)
    def _():
        own_weight().start()
        own_inputs().start()

    seed_copy().start()
    values = codes[...].astype(F32)
    tally[0] = jnp.broadcast_to(
        jnp.sum(jnp.sum(values, axis=1, keepdims=True), axis=0, keepdims=True), (8, 128)
    )
    seed_copy().wait()

    @pl.when(first)
    def _():
        row = jnp.where(half == 0, values[0:1], values[1:2])
        grid = (TOK, TOK)
        diagonal = lax.broadcasted_iota(jnp.int32, grid, 0) == lax.broadcasted_iota(
            jnp.int32, grid, 1
        )
        spread_row = jnp.broadcast_to(row, grid)
        scale = jnp.sum(jnp.where(diagonal, spread_row, 0.0), axis=1, keepdims=True) / 127.0
        for j in range(CHUNKS):
            part = staged[:, j * COLS:(j + 1) * COLS].astype(F32)
            grads[1, j] = (part * scale).astype(BF16)

    pl.semaphore_wait(barrier, 6 + (1 - core) * ((x + 3) // 4))

    def remote(src, dst, send, recv, target):
        return pltpu.make_async_remote_copy(
            src_ref=src, dst_ref=dst, send_sem=send, recv_sem=recv,
            device_id=target, device_id_type=MESH,
        )

    def lend_weight():
        return remote(
            shard.at[0], weights.at[core, here], cross_send.at[0],
            gather_recv.at[core, here], sister,
        )

    def lend_inputs():
        return remote(
            inputs.at[0, half], units.at[core], cross_send.at[1], cross_recv.at[core], sister
        )

    def cross_inputs(first_row, rows):
        part = pl.ds(first_row, rows)
        return remote(
            inputs.at[0, 1 - half, :, part], units.at[core, :, part], cross_send.at[2],
            cross_recv.at[core], device(x, far, half, y),
        )

    @pl.when(jnp.logical_not(home))
    def _():
        lend_weight().start()
        lend_inputs().start()

    def block_ref(k, yy, ll):
        return weights.at[k, yy * 8 + ll]

    def gather_z(k, ll, sgn):
        return remote(
            block_ref(k, y, ll), block_ref(k, y, ll), gather_z_send.at[(1 - sgn) // 2, k, ll],
            gather_recv.at[k, y * 8 + ll], zdev[sgn],
        )

    def gather_y(k, yy, ll, sgn, slot):
        return remote(
            block_ref(k, yy, ll), block_ref(k, yy, ll), gather_y_send.at[slot, k, ll],
            gather_recv.at[k, yy * 8 + ll], ydev[sgn],
        )

    def arrived(k, yy, ll):
        remote(
            block_ref(k, yy, ll), block_ref(k, yy, ll), cross_send.at[0],
            gather_recv.at[k, yy * 8 + ll], sister,
        ).wait_recv()

    def side(ll):
        return 1 - 2 * (ll % 2)

    def ring_place(t, sgn):
        zz = (z + 16 - sgn * t) % 16
        return zz // 8 == core, zz % 8

    def spread_y(k, ll):
        gather_y(k, y, ll, 1, 0).start()
        gather_y(k, y, ll, -1, 1).start()

    @pl.when(home)
    def _():
        own_weight().wait()

        def begin(k):
            for sgn in (1, -1):
                gather_z(k, low, sgn).start()
            spread_y(k, low)

        begin(core)
        arrived(1 - core, y, low)
        begin(1 - core)

    def relay_y(t, sgn):
        valid, ll = ring_place(t, sgn)
        valid = jnp.logical_and(valid, jnp.logical_or(t < 8, side(ll) == sgn))

        @pl.when(valid)
        def _():
            for k in (1, 0):
                arrived(k, (y + 3) % 4, ll)

                @pl.when(side(ll) == 1)
                def _():
                    gather_y(k, (y + 3) % 4, ll, 1, 2).start()

                arrived(k, (y + 1) % 4, ll)

                @pl.when(side(ll) == -1)
                def _():
                    gather_y(k, (y + 1) % 4, ll, -1, 2).start()

    def relay_z(t, sgn):
        valid, ll = ring_place(t, sgn)
        valid = jnp.logical_and(valid, jnp.logical_or(t < 8, side(ll) == sgn))
        onward = jnp.logical_or(t < 7, jnp.logical_and(t == 7, side(ll) == sgn))

        @pl.when(valid)
        def _():
            for k in (1, 0):
                arrived(k, y, ll)

                @pl.when(onward)
                def _():
                    gather_z(k, ll, sgn).start()

                spread_y(k, ll)

    def pass_tally(slot, target):
        return remote(
            tally.at[slot], tally.at[slot + 1], tally_send.at[slot], tally_recv.at[slot + 1],
            target,
        )

    pass_tally(0, zdev[1]).start()

    def tally_y(slot):
        pass_tally(slot - 1, ydev[1]).wait_recv()
        pass_tally(slot, ydev[1]).start()

    def gather_step(t, carry):
        @pl.when(core == 1)
        def _():
            cross_inputs((t - 1) * COLS, COLS).start()

        for sgn in (1, -1):
            relay_z(t, sgn)

        @pl.when(t == 1)
        def _():
            relay_y(0, 1)

        @pl.when(t > 1)
        def _():
            for sgn in (1, -1):
                relay_y(t - 1, sgn)

        @pl.when(t < 7)
        def _():
            pass_tally(t - 1, zdev[1]).wait_recv()
            pass_tally(t, zdev[1]).start()

        return carry

    lax.fori_loop(1, 9, gather_step, 0)

    @pl.when(core == 0)
    def _():
        cross_inputs(0, WIDTH).start()

    for sgn in (1, -1):
        relay_y(8, sgn)

    pass_tally(6, zdev[1]).wait_recv()
    tally[8] = sum(tally[i] for i in range(1, 8)) + tally[0]
    pass_tally(8, ydev[1]).start()

    def ready(k):
        local = jnp.logical_and(home, core == k)

        @pl.when(local)
        def _():
            own_inputs().wait()

        @pl.when(jnp.logical_not(local))
        def _():
            remote(
                units.at[k], units.at[k], cross_send.at[1], cross_recv.at[k], sister
            ).wait_recv()

    def far_arrived(ll, carry):
        for k in (1, 0):
            arrived(k, (y + 2) % 4, ll)
        return carry

    lax.fori_loop(0, 8, far_arrived, 0)

    def weight_chunk(k, j):
        return weights[k, j * GROUPS:(j + 1) * GROUPS].reshape(COLS, HIDDEN)

    def columns(ref, k, j):
        return ref[k, :, j * COLS:(j + 1) * COLS]

    def unrolled(body, carry):
        for j in range(CHUNKS):
            carry = body(j, carry)
        return carry

    def flip(k):
        for j in range(CHUNKS):
            flipped[k, j] = weight_chunk(k, j).T

    def prepare(k):
        ready(k)

        def square(j, acc):
            v = columns(units, k, j).astype(F32)
            return acc + jnp.sum(v * v, axis=-1, keepdims=True)

        total = unrolled(square, jnp.zeros((TOK, 1), F32))
        inv = lax.rsqrt(total / WIDTH + EPSILON)
        inv_rms[k] = jnp.broadcast_to(inv, (TOK, 128))

        def multiply(j, acc):
            row = (columns(units, k, j).astype(F32) * inv).astype(BF16)
            normed[k, :, j * COLS:(j + 1) * COLS] = row
            return acc + jnp.dot(row, weight_chunk(k, j), preferred_element_type=F32)

        value = unrolled(multiply, jnp.zeros((TOK, HIDDEN), F32))
        prob = jax.nn.sigmoid(value)
        project[k] = value
        slope[k] = prob * (1.0 + value * (1.0 - prob))
        factors[k, TOK:] = (value * prob).astype(BF16)

    prepare(1)

    @pl.when(jnp.logical_not(first))
    def _():
        flip(1)
        flip(0)
        prepare(0)

    def rows_of(w):
        return slice(w * PART, (w + 1) * PART)

    def chain(w, j, target):
        part = pl.ds(w * PART, PART)
        return remote(
            outgoing.at[j, part], grads.at[1, j, part], chain_send.at[w, j],
            chain_recv.at[w, j], target,
        )

    def stage(k, w):
        part = rows_of(w)

        def act_grad(j, acc):
            if k == 1:
                @pl.when(jnp.logical_not(first))
                def _():
                    chain(w, j, sister).wait_recv()
            return acc + jnp.dot(
                grads[k, j, part], weight_chunk(k, j), preferred_element_type=F32
            )

        grad_act = unrolled(act_grad, jnp.zeros((PART, HIDDEN), F32))
        grad_proj = (grad_act * slope[k, part]).astype(BF16)
        factors[k, part] = grad_proj
        mean = jnp.sum(grad_proj.astype(F32) * project[k, part], axis=-1, keepdims=True) / WIDTH
        inv = inv_rms[k, part, 0:1]

        def straight(j):
            return lax.dot_general(
                grad_proj, weight_chunk(k, j), (((1,), (1,)), ((), ())),
                preferred_element_type=F32,
            )

        def turned(j):
            return jnp.dot(grad_proj, flipped[k, j], preferred_element_type=F32)

        def in_grad(j, product):
            norm = product(j)
            unit = units[k, part, j * COLS:(j + 1) * COLS].astype(F32) * inv
            result = (grads[k, j, part].astype(F32) + inv * (norm - unit * mean)).astype(BF16)
            if k == 1:
                grads[0, j, part] = result
            else:
                outgoing[j, part] = result

                @pl.when(core == 1)
                def _():
                    chain(w, j, sister).start()

                @pl.when(core == 0)
                def _():
                    chain(w, j, next_x).start()

            return product

        @pl.when(first)
        def _():
            unrolled(in_grad, straight)

        @pl.when(jnp.logical_and(jnp.logical_not(first), jnp.logical_or(k == 1, jnp.logical_not(last))))
        def _():
            unrolled(in_grad, turned)

    stage(1, 0)

    @pl.when(first)
    def _():
        prepare(0)

    stage(0, 0)
    tally_y(9)
    stage(1, 1)
    stage(0, 1)
    tally_y(10)

    def weight_grad(k):
        def rows(j, carry):
            left = jnp.concatenate([columns(normed, k, j), grads[k, j]], axis=0)
            term = lax.dot_general(
                left, factors[k], (((0,), (0,)), ((), ())), preferred_element_type=F32
            )
            term = term.astype(BF16)
            for i in range(GROUPS):
                place = j * GROUPS + i
                block = term[i * ROWS:(i + 1) * ROWS]
                partial[k, place] = block[:, :SPLIT]
                wide[k, place % 8, place // 8] = block[:, SPLIT:]
            return carry

        unrolled(rows, 0)

    def part_ref(k, dy, ll):
        return partial.at[k, ((y + 4 + dy) % 4) * 8 + ll]

    def send_hop1(k, ll, sgn):
        return remote(
            part_ref(k, 2, ll), hop1.at[k, ll], sum_y_send.at[0, k, ll], hop1_recv.at[k, ll],
            ydev[sgn],
        )

    def send_hop2(k, ll, sgn):
        land, sem = (hop2p, hop2p_recv) if sgn == 1 else (hop2m, hop2m_recv)
        return remote(
            part_ref(k, sgn, ll), land.at[k, ll], sum_y_send.at[(3 - sgn) // 2, k, ll],
            sem.at[k, ll], ydev[sgn],
        )

    def send_ring(k, ll, sgn):
        land, sem = (ringp, ringp_recv) if sgn == 1 else (ringm, ringm_recv)
        return remote(
            part_ref(k, 0, ll), land.at[k, ll], sum_z_send.at[k, ll], sem.at[k, ll], zdev[sgn]
        )

    def target_place(t, sgn):
        zz = (z + 16 + sgn * t) % 16
        ll = zz % 8
        valid = jnp.logical_and(zz // 8 == core, jnp.logical_or(t < 8, side(ll) == sgn))
        return valid, ll

    def begin_y(k, t, sgn):
        valid, ll = target_place(t, sgn)

        @pl.when(valid)
        def _():
            @pl.when(side(ll) == 1)
            def _():
                send_hop1(k, ll, 1).start()
                send_hop2(k, ll, -1).start()

            @pl.when(side(ll) == -1)
            def _():
                send_hop1(k, ll, -1).start()
                send_hop2(k, ll, 1).start()

    def begin_sum(k):
        def body(i, carry):
            for sgn in (1, -1):
                begin_y(k, 8 - i, sgn)
            return carry

        lax.fori_loop(0, AHEAD, body, 0)

    def add_into(k, dy, ll, extra):
        index = ((y + 4 + dy) % 4) * 8 + ll
        value = partial[k, index].astype(F32)
        for ref in extra:
            value = value + ref[k, ll].astype(F32)
        partial[k, index] = value.astype(BF16)

    def middle_y(t, sgn):
        valid, ll = target_place(t, sgn)

        @pl.when(valid)
        def _():
            for k in (1, 0):
                send_hop1(k, ll, 1).wait_recv()

                @pl.when(side(ll) == 1)
                def _():
                    add_into(k, 1, ll, (hop1,))
                    send_hop2(k, ll, 1).start()

                @pl.when(side(ll) == -1)
                def _():
                    add_into(k, -1, ll, (hop1,))
                    send_hop2(k, ll, -1).start()

    def ring_sum(t, sgn):
        valid, ll = target_place(t, sgn)
        fed = jnp.logical_or(t < 7, jnp.logical_and(t == 7, side(ll) == sgn))
        land = ringp if sgn == 1 else ringm

        @pl.when(valid)
        def _():
            for k in (1, 0):
                send_hop2(k, ll, 1).wait_recv()
                send_hop2(k, ll, -1).wait_recv()

                @pl.when(fed)
                def _():
                    send_ring(k, ll, sgn).wait_recv()
                    add_into(k, 0, ll, (hop2p, hop2m, land))

                @pl.when(jnp.logical_not(fed))
                def _():
                    add_into(k, 0, ll, (hop2p, hop2m))

                send_ring(k, ll, sgn).start()

    def send_wide(k, ll, sgn):
        land, sem = (widep, widep_recv) if sgn == 1 else (widem, widem_recv)
        return remote(
            wide.at[k, ll], land.at[k, ll], wide_send.at[k, ll], sem.at[k, ll], zdev[sgn]
        )

    def ring_wide(t, sgn):
        valid, ll = target_place(t, sgn)
        fed = jnp.logical_or(t < 7, jnp.logical_and(t == 7, side(ll) == sgn))
        land = widep if sgn == 1 else widem

        @pl.when(valid)
        def _():
            for k in (1, 0):
                @pl.when(fed)
                def _():
                    send_wide(k, ll, sgn).wait_recv()
                    wide[k, ll] = (wide[k, ll].astype(F32) + land[k, ll].astype(F32)).astype(BF16)

                send_wide(k, ll, sgn).start()

    def end_ref(k, dy):
        return wide.at[k, low, (y + 4 + dy) % 4]

    def send_end1(k):
        sgn = 2 * k - 1
        return remote(end_ref(k, 2), end1.at[k], end_send.at[0, k], end1_recv.at[k], ydev[sgn])

    def send_end2(k, sgn):
        land, sem = (end2p, end2p_recv) if sgn == 1 else (end2m, end2m_recv)
        return remote(
            end_ref(k, sgn), land.at[k], end_send.at[(3 - sgn) // 2, k], sem.at[k], ydev[sgn]
        )

    def end_wide():
        for k in (1, 0):
            send_wide(k, low, 1).wait_recv()
            send_wide(k, low, -1).wait_recv()
            value = wide[k, low].astype(F32)
            for ref in (widep, widem):
                value = value + ref[k, low].astype(F32)
            wide[k, low] = value.astype(BF16)
            send_end1(k).start()
            send_end2(k, 1 - 2 * k).start()

    def end_wide_later():
        for k in (1, 0):
            sgn = 2 * k - 1
            send_end1(k).wait_recv()
            place = (y + 4 + sgn) % 4
            value = wide[k, low, place].astype(F32) + end1[k].astype(F32)
            wide[k, low, place] = value.astype(BF16)
            send_end2(k, sgn).start()

    for k in (1, 0):
        weight_grad(k)
        begin_sum(k)

    def sum_step(i, carry):
        @pl.when(i < 8)
        def _():
            for sgn in (1, -1):
                ring_wide(8 - i, sgn)
            for sgn in (1, -1):
                middle_y(8 - i, sgn)

        pl.when(jnp.logical_and(i == 8, home))(end_wide)

        @pl.when(i == 8)
        def _():
            middle_y(0, 1)

        @pl.when(jnp.logical_and(i >= 1, i < 9))
        def _():
            for sgn in (1, -1):
                ring_sum(9 - i, sgn)

        later = 8 - AHEAD - i

        @pl.when(later >= 1)
        def _():
            for k in (1, 0):
                for sgn in (1, -1):
                    begin_y(k, later, sgn)

        @pl.when(later == 0)
        def _():
            for k in (1, 0):
                begin_y(k, 0, 1)

        return carry

    lax.fori_loop(0, 9, sum_step, 0)
    pl.when(home)(end_wide_later)

    pass_tally(10, ydev[1]).wait_recv()
    scale = 127.0 / sum(tally[i] for i in range(8, 12))[0:1, 0:1]

    def send_final():
        return remote(final.at[0], final.at[1], final_send.at[0], final_recv.at[0], sister)

    @pl.when(home)
    def _():
        def total(k, put):
            for sgn in (1, -1):
                send_hop2(k, low, sgn).wait_recv()
                send_ring(k, low, sgn).wait_recv()
            value = partial[k, here].astype(F32)
            for ref in (hop2p, hop2m, ringp, ringm):
                value = value + ref[k, low].astype(F32)
            send_end2(k, 1).wait_recv()
            send_end2(k, -1).wait_recv()
            rest = wide[k, low, y].astype(F32)
            for ref in (end2p, end2m):
                rest = rest + ref[k].astype(F32)
            put[0, :, :SPLIT] = value * scale
            put[0, :, SPLIT:] = rest * scale

        total(1 - core, final)
        send_final().start()
        total(core, out)
        send_final().wait_send()

    @pl.when(jnp.logical_not(home))
    def _():
        send_final().wait_recv()
        out[0] = final[1]

    @pl.when(jnp.logical_not(home))
    def _():
        lend_weight().wait_send()
        lend_inputs().wait_send()

    cross_inputs(0, WIDTH).wait_send()

    @pl.when(jnp.logical_not(last))
    def _():
        for w in range(WAVES):
            for j in range(CHUNKS):
                chain(w, j, sister).wait_send()

    for i in (0, 1, 2, 3, 4, 5, 6, 8, 9, 10):
        pass_tally(i, sister).wait_send()

    @pl.when(home)
    def _():
        for k in (1, 0):
            send_end1(k).wait_send()
            send_end2(k, 1).wait_send()
            send_end2(k, -1).wait_send()

    def settle(ll, carry):
        zz = core * 8 + ll
        ahead = (z + 16 - zz) % 16
        plus = jnp.logical_or(ahead < 7, jnp.logical_and(ahead == 7, side(ll) == 1))
        back = (16 - ahead) % 16
        minus = jnp.logical_or(back < 7, jnp.logical_and(back == 7, side(ll) == -1))
        for k in (1, 0):
            @pl.when(plus)
            def _():
                gather_z(k, ll, 1).wait_send()

            @pl.when(minus)
            def _():
                gather_z(k, ll, -1).wait_send()

            gather_y(k, y, ll, 1, 0).wait_send()
            gather_y(k, y, ll, -1, 1).wait_send()
            gather_y(k, y, ll, 1, 2).wait_send()
            send_hop1(k, ll, 1).wait_send()
            send_hop2(k, ll, 1).wait_send()
            send_hop2(k, ll, -1).wait_send()

            @pl.when(ahead != 0)
            def _():
                send_ring(k, ll, 1).wait_send()
                send_wide(k, ll, 1).wait_send()

        return carry

    lax.fori_loop(0, 8, settle, 0)


def shards(section_inputs, loss_grads, weight_codes, proj_weight):
    anywhere = pl.BlockSpec(memory_space=pl.ANY)
    vmem = pl.BlockSpec(memory_space=pltpu.VMEM)
    dma = pltpu.SemaphoreType.DMA
    blocks = (2, 8, ROWS, SPLIT)
    slabs = (2, 8, 4, ROWS, REST)
    ends = (2, ROWS, REST)
    return pl.pallas_call(
        kernel,
        out_shape=jax.ShapeDtypeStruct((1, ROWS, HIDDEN), F32),
        in_specs=[anywhere, anywhere, vmem, vmem],
        out_specs=vmem,
        scratch_shapes=[
            pltpu.VMEM((2, 32, ROWS, HIDDEN), BF16),
            pltpu.VMEM((2, TOK, WIDTH), BF16),
            pltpu.VMEM((2, TOK, WIDTH), BF16),
            pltpu.VMEM((2, CHUNKS, TOK, COLS), BF16),
            pltpu.VMEM((CHUNKS, TOK, COLS), BF16),
            pltpu.VMEM((2, 2 * TOK, HIDDEN), BF16),
            pltpu.VMEM((2, TOK, HIDDEN), F32),
            pltpu.VMEM((2, TOK, HIDDEN), F32),
            pltpu.VMEM((2, TOK, 128), F32),
            pltpu.VMEM((2, CHUNKS, HIDDEN, COLS), BF16),
            pltpu.VMEM((2, 32, ROWS, SPLIT), BF16),
            pltpu.VMEM(slabs, BF16),
            pltpu.VMEM(blocks, BF16),
            pltpu.VMEM(blocks, BF16),
            pltpu.VMEM(blocks, BF16),
            pltpu.VMEM(blocks, BF16),
            pltpu.VMEM(blocks, BF16),
            pltpu.VMEM(slabs, BF16),
            pltpu.VMEM(slabs, BF16),
            pltpu.VMEM(ends, BF16),
            pltpu.VMEM(ends, BF16),
            pltpu.VMEM(ends, BF16),
            pltpu.VMEM((2, ROWS, HIDDEN), F32),
            pltpu.VMEM((12, 8, 128), F32),
            pltpu.VMEM((TOK, WIDTH), BF16),
            dma((3,)),
            dma((2, 32)),
            dma((2, 2, 8)),
            dma((3, 2, 8)),
            dma((3,)),
            dma((2,)),
            dma((WAVES, CHUNKS)),
            dma((WAVES, CHUNKS)),
            dma((2, 8)),
            dma((2, 8)),
            dma((2, 8)),
            dma((2, 8)),
            dma((2, 8)),
            dma((2, 8)),
            dma((2, 8)),
            dma((2,)),
            dma((2,)),
            dma((2,)),
            dma((2, 8)),
            dma((3, 2)),
            dma((3, 2, 8)),
            dma((2, 8)),
            dma((1,)),
            dma((1,)),
            dma((12,)),
            dma((12,)),
        ],
        compiler_params=pltpu.CompilerParams(
            collective_id=0, has_side_effects=True, vmem_limit_bytes=56 * 2**20
        ),
    )(section_inputs[0][None], loss_grads, weight_codes, proj_weight)


def solution(mesh):
    return jax.shard_map(
        shards,
        mesh=mesh,
        in_specs=(
            P("section", None, "dp", None),
            P(None, "dp", None),
            P(None, "dp"),
            P("section", "dp", None),
        ),
        out_specs=P("section", "dp", None),
        check_vma=False,
    )
```
